256 devices in a mesh: dp: 16 (over z_hi, y, core), expert: 16 (over x, z_lo).
Axes of the slice: x: 4, y: 4, z: 8 (z_hi: 2, z_lo: 4; z = z_hi * 4 + z_lo), core: 2. Of those that a mesh axis runs over, the one named last changes fastest.
Arguments:
- layer_inputs: bfloat16 [32768, 2560], P(('dp', 'expert')), may hold values from -6 to 6
- cotangent: bfloat16 [32768, 2560], P(('dp', 'expert')), may hold values from -3 to 3
- expert_ids: int32 [32768, 3], P(('dp', 'expert')), may hold values from 0 to 15, all different within a row; in each aligned block of 128 rows (0 to 127, 128 to 255, ...) at most 26 rows name the same one
- route_weights: bfloat16 [32768, 3], P(('dp', 'expert')), may hold values from 0.049804688 to 0.59765625
- w_gate_up: bfloat16 [16, 2560, 1536], P('expert'), may hold values from -0.125 to 0.125
- w_down: bfloat16 [16, 768, 2560], P('expert', None, 'dp'), may hold values from -0.21875 to 0.21875
Outputs:
- input_grad: bfloat16 [32768, 2560], P(('dp', 'expert'))
- gate_grad: bfloat16 [32768, 3], P(('dp', 'expert'))
- grad_gate_up: bfloat16 [16, 2560, 1536], P('expert', 'dp')
- grad_down: bfloat16 [16, 768, 2560], P('expert', None, 'dp')
The draws below stay inside these ranges and needn't reach their ends.
Inputs may be any that keep to these rules, and one draw needn't show every extreme that they name: `expert_ids`: each row names 3 different experts; among the rows of one device no expert is named by more than 26 rows.
All inputs are finite; a program needn't handle non-finite values.
Results may differ from the reference program's by a relative error of at most 0.019.
Values may be sent and summed in bfloat16 or wider, within the bound.
No kernel may reach another device: no remote copies, remote signals or barrier semaphores. Data moves between devices by JAX's collectives and lax.ppermute only.
A program may use at most 128 MiB of HBM per device.

```python
import math
import jax
import jax.numpy as jnp
import numpy as np
from jax import lax

D = 2560
HID = 768
TOPK = 3
TOK_DEV = 128
EXPERTS = 16
CAP = 26
GROUP_TOK = 2048
TOKENS = 32768
N_DP = 16
N_EXPERT = 16


def block_scale(stream_key, extent, pieces, smallest, top_value):
    def one(position, parts):
        heights = jax.random.uniform(jax.random.fold_in(jax.random.fold_in(stream_key, 6), position), (parts,), jnp.float32, smallest / len(pieces), top_value / len(pieces))
        return jnp.repeat(jnp.exp(heights), extent[position] // parts).reshape((-1,) + (1,) * (len(extent) - position - 1))

    level = one(*pieces[0])
    for cut in pieces[1:]:
        level = level * one(*cut)
    return level


def shared_out(key, own, number, rows, amount, top, most, skew):
    sequence = jax.random.permutation(key, amount)
    heavy_load, usual = portions_of(amount, rows * top, most, skew, True), portions_of(amount, rows * top, most, skew, False)
    places = jnp.arange(amount)

    def named(lengths, offset_by):
        used = int((lengths > 0).sum())
        fixed = max(1, used // 4)
        shifted = fixed + (places - fixed + offset_by * (used - fixed)) % max(1, amount - fixed)
        return jnp.zeros((amount,), jnp.int32).at[sequence[jnp.where(places < fixed, places, shifted)]].set(jnp.asarray(lengths, jnp.int32))

    lengths = jnp.where(number % 4 == 0, named(heavy_load, number // 4), named(usual, number - number // 4 - 1))
    mixed = jax.random.permutation(jax.random.fold_in(own, 3), amount)
    giver, receiver = mixed[0:amount // 2 * 2:2], mixed[1:amount // 2 * 2:2]
    margin = jnp.minimum(lengths[giver] - 1, most - lengths[receiver]) // 2
    margin = jnp.where((giver == sequence[0]) | (receiver == sequence[0]) | (lengths[receiver] == 0), 0, jnp.maximum(margin, 0))
    shifted = jax.random.randint(jax.random.fold_in(own, 4), (amount // 2,), 0, 1 << 20) % (margin + 1)
    lengths = lengths.at[giver].add(-shifted).at[receiver].add(shifted)
    labels = jnp.searchsorted(jnp.cumsum(lengths), jnp.arange(rows * top), side="right").astype(jnp.int32)
    listing = labels.reshape(top, rows).T
    listing = listing[jax.random.permutation(jax.random.fold_in(own, 1), rows)]
    offset_by = jax.random.randint(jax.random.fold_in(own, 2), (rows, 1), 0, top)
    return jnp.take_along_axis(listing, (jnp.arange(top)[None, :] + offset_by) % top, axis=1)


def portions_of(amount, total, limit, slope, full):
    weights = [(1 << 20) // math.isqrt(rank ** slope) + 1 for rank in range(1, amount + 1)]
    largest = limit if full else min(limit, max(-(-total // amount), total * weights[0] // sum(weights)))
    least = 1 if total - largest >= amount - 1 else 0
    holding, spare = [largest] + [least] * (amount - 1), total - largest - least * (amount - 1)
    while spare > 0:
        candidates = [i for i in range(1, amount) if holding[i] < largest] or [i for i in range(1, amount) if holding[i] < limit]
        pool, remaining = sum([weights[i] for i in candidates]), spare
        for i in candidates:
            more = min(limit - holding[i], max(1, remaining * weights[i] // pool), spare)
            holding[i] = holding[i] + more
            spare = spare - more
    return np.array(holding)


def gaussian(own_key, shape, spread, reach, shards=(), kind=jnp.bfloat16):
    factor_of = block_scale(own_key, shape, shards, -0.22, 0.18) if shards else 1.0
    entries = jax.random.normal(own_key, shape, jnp.float32) * spread * factor_of
    return jnp.minimum(jnp.maximum(entries, -reach), reach).astype(kind)


def setup_inputs(seed: int = 0) -> dict:
    splits = jax.random.split(jax.random.key(seed), 7)
    layer_inputs = gaussian(splits[0], (TOKENS, D), 1.0, 6.0, ((0, 256),))
    cotangent = gaussian(splits[1], (TOKENS, D), 0.5, 3.0, ((0, 256),))
    expert_ids_keys = jax.random.split(jax.random.fold_in(splits[2], 1), TOKENS // TOK_DEV)
    expert_ids_turns = jax.random.permutation(jax.random.fold_in(splits[2], 3), TOKENS // TOK_DEV)
    expert_ids = jax.vmap(lambda own, number: shared_out(jax.random.fold_in(splits[2], 2), own, number, TOK_DEV, EXPERTS, TOPK, CAP, 2))(expert_ids_keys, expert_ids_turns).reshape((TOKENS, TOPK))
    route_weights = jnp.clip(jnp.exp(math.log(0.59765625) - 2.4849066 * jax.random.uniform(splits[3], (TOKENS, TOPK), jnp.float32) ** block_scale(splits[3], (TOKENS, TOPK), ((0, 256),), -0.2, 0.2)), 0.049804688, 0.59765625).astype(jnp.bfloat16)
    w_gate_up = gaussian(splits[4], (EXPERTS, D, 2 * HID), D ** -0.5, 0.125, ((0, 16),))
    w_down = gaussian(splits[5], (EXPERTS, HID, D), HID ** -0.5, 0.21875, ((0, 16), (2, 16)))
    return {"layer_inputs": layer_inputs, "cotangent": cotangent, "expert_ids": expert_ids, "route_weights": route_weights, "w_gate_up": w_gate_up, "w_down": w_down}


def expert_pass(expert_rows, expert_cot, expert_gate, gate_up, down_proj):
    projected = jnp.dot(expert_rows, gate_up, preferred_element_type=jnp.float32)
    gate_pre = projected[:, :HID]
    up_pre = projected[:, HID:]
    sigmoid_gate = jax.nn.sigmoid(gate_pre)
    silu_gate = gate_pre * sigmoid_gate
    hidden = (silu_gate * up_pre).astype(jnp.bfloat16)
    expert_out = jnp.dot(hidden, down_proj, preferred_element_type=jnp.float32)
    gate_dot = jnp.sum(expert_cot.astype(jnp.float32) * expert_out, axis=1)
    out_grad = (expert_gate.astype(jnp.float32)[:, None] * expert_cot.astype(jnp.float32)).astype(jnp.bfloat16)
    hidden_grad = lax.dot_general(out_grad, down_proj, (((1,), (1,)), ((), ())), preferred_element_type=jnp.float32)
    pre_grad = jnp.concatenate([hidden_grad * up_pre * sigmoid_gate * (1.0 + gate_pre * (1.0 - sigmoid_gate)), hidden_grad * silu_gate], axis=1).astype(jnp.bfloat16)
    row_grads = lax.dot_general(pre_grad, gate_up, (((1,), (1,)), ((), ())), preferred_element_type=jnp.float32).astype(jnp.bfloat16)
    gu_grad = lax.dot_general(expert_rows, pre_grad, (((0,), (0,)), ((), ())), preferred_element_type=jnp.float32)
    down_grad = lax.dot_general(hidden, out_grad, (((0,), (0,)), ((), ())), preferred_element_type=jnp.float32)
    return row_grads, gate_dot, gu_grad, down_grad


def per_expert(operands):
    return expert_pass(operands[0], operands[1], operands[2], operands[3], operands[4])


def reference(layer_inputs, cotangent, expert_ids, route_weights, w_gate_up, w_down):
    pair_count = GROUP_TOK * TOPK
    slot_count = N_EXPERT * CAP
    rows_all = layer_inputs.reshape(N_DP, GROUP_TOK, D)
    cot_all = cotangent.reshape(N_DP, GROUP_TOK, D)
    ids_all = expert_ids.reshape(N_DP, GROUP_TOK, TOPK)
    gate_all = route_weights.reshape(N_DP, GROUP_TOK, TOPK)

    def group_step(carry, group_item):
        acc_gu, acc_down = carry
        group_rows, group_cot, group_ids, group_gate = group_item
        chosen_ids = group_ids.reshape(N_EXPERT, TOK_DEV * TOPK)
        one_hot = (chosen_ids[:, :, None] == jnp.arange(EXPERTS, dtype=jnp.int32)[None, None, :]).astype(jnp.int32)
        pair_rank = jnp.sum((jnp.cumsum(one_hot, axis=1) - one_hot) * one_hot, axis=2)
        source_dev = jnp.arange(N_EXPERT, dtype=jnp.int32)[:, None]
        pair_slot = (source_dev * CAP + pair_rank).reshape(-1).astype(jnp.int32)
        pair_dest = chosen_ids.reshape(-1).astype(jnp.int32)
        token_index = (jnp.arange(pair_count, dtype=jnp.int32) // TOPK).astype(jnp.int32)
        rows_buf = jnp.zeros((EXPERTS, slot_count, D), jnp.bfloat16).at[pair_dest, pair_slot].set(group_rows[token_index])
        cot_buf = jnp.zeros((EXPERTS, slot_count, D), jnp.bfloat16).at[pair_dest, pair_slot].set(group_cot[token_index])
        gate_buf = jnp.zeros((EXPERTS, slot_count), jnp.bfloat16).at[pair_dest, pair_slot].set(group_gate.reshape(-1))
        row_grads, gate_dot, gu_grad, down_grad = lax.map(per_expert, (rows_buf, cot_buf, gate_buf, w_gate_up, w_down))
        acc_gu = acc_gu + lax.optimization_barrier(gu_grad.astype(jnp.bfloat16)).astype(jnp.float32)
        acc_down = acc_down + lax.optimization_barrier(down_grad.astype(jnp.bfloat16)).astype(jnp.float32)
        pair_grads = row_grads[pair_dest, pair_slot].astype(jnp.float32).reshape(GROUP_TOK, TOPK, D)
        token_grads = jnp.sum(pair_grads, axis=1).astype(jnp.bfloat16)
        pair_dots = gate_dot[pair_dest, pair_slot].reshape(GROUP_TOK, TOPK).astype(jnp.bfloat16)
        return (acc_gu, acc_down), (token_grads, pair_dots)

    start_gu = jnp.zeros((EXPERTS, D, 2 * HID), jnp.float32)
    start_down = jnp.zeros((EXPERTS, HID, D), jnp.float32)
    (acc_gu, acc_down), (token_grads, pair_dots) = lax.scan(group_step, (start_gu, start_down), (rows_all, cot_all, ids_all, gate_all))
    input_grad = token_grads.reshape(TOKENS, D)
    gate_grad = pair_dots.reshape(TOKENS, TOPK)
    return input_grad, gate_grad, acc_gu.astype(jnp.bfloat16), acc_down.astype(jnp.bfloat16)
```

```python
import jax
import jax.numpy as jnp
from jax import lax
from jax.sharding import PartitionSpec as P


def on_device(layer_inputs, cotangent, expert_ids, route_weights, w_gate_up, w_down):
    tok_rows, feat_width = layer_inputs.shape
    top_count = expert_ids.shape[1]
    expert_count = lax.axis_size("expert")
    capacity = tok_rows * top_count // expert_count * 13 // 12
    pair_count = tok_rows * top_count
    slot_total = expert_count * capacity
    hidden_width = w_down.shape[1]
    chosen_ids = expert_ids.reshape(-1)
    order = jnp.arange(pair_count, dtype=jnp.int32)
    earlier = (chosen_ids[:, None] == chosen_ids[None, :]) & (order[None, :] < order[:, None])
    pair_rank = jnp.sum(earlier.astype(jnp.int32), axis=1)
    pair_slot = chosen_ids * capacity + pair_rank
    slot_owner = (
        jnp.full((slot_total,), -1, jnp.int32)
        .at[pair_slot]
        .set(jnp.arange(pair_count, dtype=jnp.int32))
    )
    filled = slot_owner >= 0
    owner_safe = jnp.where(filled, slot_owner, 0)
    source_token = owner_safe // top_count
    zero_bf = jnp.zeros((), jnp.bfloat16)
    rows_out = jnp.where(filled[:, None], layer_inputs[source_token], zero_bf).reshape(
        expert_count, capacity, feat_width
    )
    cot_out = jnp.where(filled[:, None], cotangent[source_token], zero_bf).reshape(
        expert_count, capacity, feat_width
    )
    gate_out = jnp.where(filled, route_weights.reshape(-1)[owner_safe], zero_bf).reshape(
        expert_count, capacity
    )
    rows_in, cot_in, gate_in = (
        lax.all_to_all(rows_out, "expert", split_axis=0, concat_axis=0, tiled=True),
        lax.all_to_all(cot_out, "expert", split_axis=0, concat_axis=0, tiled=True),
        lax.all_to_all(gate_out, "expert", split_axis=0, concat_axis=0, tiled=True),
    )
    expert_rows = rows_in.reshape(slot_total, feat_width)
    gate_up = w_gate_up[0]
    projected = jnp.dot(expert_rows, gate_up, preferred_element_type=jnp.float32)
    gate_pre = projected[:, :hidden_width]
    up_pre = projected[:, hidden_width:]
    sigmoid_gate = jax.nn.sigmoid(gate_pre)
    silu_gate = gate_pre * sigmoid_gate
    hidden = (silu_gate * up_pre).astype(jnp.bfloat16)
    expert_cot = cot_in.reshape(slot_total, feat_width)
    expert_gate = gate_in.reshape(slot_total)
    out_grad = (expert_gate.astype(jnp.float32)[:, None] * expert_cot.astype(jnp.float32)).astype(
        jnp.bfloat16
    )
    col_block = lax.all_gather(w_down, "dp", axis=2, tiled=True)[0]
    out_part = jnp.dot(hidden, col_block, preferred_element_type=jnp.float32)
    gate_dot = jnp.sum(expert_cot.astype(jnp.float32) * out_part, axis=1)
    hidden_grad = lax.dot_general(
        out_grad, col_block, (((1,), (1,)), ((), ())), preferred_element_type=jnp.float32
    )
    gate_dot, hidden_grad = (gate_dot, hidden_grad)
    pre_grad = jnp.concatenate(
        [
            hidden_grad * up_pre * sigmoid_gate * (1.0 + gate_pre * (1.0 - sigmoid_gate)),
            hidden_grad * silu_gate,
        ],
        axis=1,
    ).astype(jnp.bfloat16)
    row_grads = lax.dot_general(
        pre_grad, gate_up, (((1,), (1,)), ((), ())), preferred_element_type=jnp.float32
    ).astype(jnp.bfloat16)
    back_rows, back_dots = (
        lax.all_to_all(
            row_grads.reshape(expert_count, capacity, feat_width),
            "expert",
            split_axis=0,
            concat_axis=0,
            tiled=True,
        ),
        lax.all_to_all(
            gate_dot.astype(jnp.bfloat16).reshape(expert_count, capacity),
            "expert",
            split_axis=0,
            concat_axis=0,
            tiled=True,
        ),
    )
    pair_grads = (
        back_rows.reshape(slot_total, feat_width)[pair_slot]
        .astype(jnp.float32)
        .reshape(tok_rows, top_count, feat_width)
    )
    input_grad = jnp.sum(pair_grads, axis=1).astype(jnp.bfloat16)
    gate_grad = back_dots.reshape(-1)[pair_slot].reshape(tok_rows, top_count)
    gu_grad = lax.psum_scatter(
        lax.dot_general(
            expert_rows, pre_grad, (((0,), (0,)), ((), ())), preferred_element_type=jnp.float32
        ).astype(jnp.bfloat16),
        "dp",
        scatter_dimension=0,
        tiled=True,
    )
    down_local = lax.dot_general(
        hidden, out_grad, (((0,), (0,)), ((), ())), preferred_element_type=jnp.float32
    )
    down_grad = lax.psum_scatter(
        down_local.astype(jnp.bfloat16), "dp", scatter_dimension=1, tiled=True
    )
    return (input_grad, gate_grad, gu_grad[None], down_grad[None])


def solution(mesh):
    placed = (
        P(("dp", "expert"), None),
        P(("dp", "expert"), None),
        P(("dp", "expert"), None),
        P(("dp", "expert"), None),
        P("expert", None, None),
        P("expert", None, "dp"),
    )
    return jax.shard_map(
        on_device,
        mesh=mesh,
        in_specs=placed,
        out_specs=(
            P(("dp", "expert"), None),
            P(("dp", "expert"), None),
            P("expert", "dp", None),
            P("expert", None, "dp"),
        ),
        check_vma=False,
    )
```

```python
import functools

import jax
import jax.numpy as jnp
import numpy as np
from jax import lax
from jax.experimental import pallas as pl
from jax.experimental.pallas import tpu as pltpu
from jax.sharding import Mesh
from jax.sharding import PartitionSpec as P

AXES = ("zh", "y", "c", "x", "zl")
SIZES = (2, 4, 2, 4, 4)
CAP = 26
BLOCK = 4 * CAP
SLOTS = 16 * CAP
BF = jnp.bfloat16
F32 = jnp.float32
PLACE = {(2, 0): 0, (1, 1): 1, (2, 1): 2, (3, 0): 3, (1, 0): 4, (3, 1): 5, (0, 0): 6, (0, 1): 7}


def pairs_of(move):
    out = []
    for i in range(int(np.prod(SIZES))):
        zh, y, c, x, zl = (int(v) for v in np.unravel_index(i, SIZES))
        z, y, c, x = move(zh * 4 + zl, y, c, x)
        z, y, c, x = z % 8, y % 4, c % 2, x % 4
        out.append((i, int(np.ravel_multi_index((z // 4, y, c, x, z % 4), SIZES))))
    return out


def shift(dz=0, dy=0, dc=0, dx=0):
    return pairs_of(lambda z, y, c, x: (z + dz, y + dy, c + dc, x + dx))


def z_window(d):
    if d == 2:
        return pairs_of(lambda z, y, c, x: (z + 2 - 4 * (z % 2), y, c, x))
    return shift(dz=1 if d == 1 else -1)


def back(pairs):
    return [(b, a) for a, b in pairs]


def send(v, pairs):
    return lax.ppermute(v, AXES, pairs)


def expert_at(pos, d, dx):
    return lax.rem(pos[0] + dx, 4) * 4 + lax.rem(pos[1] + d, 4)


def prep_kernel(pos, ids, w, xin, cot, *refs):
    rows, ogs, sel1_out, sel2_out = refs[:4], refs[4:8], refs[8], refs[9]
    rank_s, wt_s, s1, s2, sw2 = refs[10:]
    tok = ids.shape[1]
    eid = lax.broadcasted_iota(jnp.int32, (16, tok), 0)
    member = jnp.zeros((16, tok), F32)
    weight = jnp.zeros((16, tok), F32)
    for k in range(3):
        hit = eid == ids[k : k + 1, :]
        member = member + jnp.where(hit, 1.0, 0.0)
        weight = weight + jnp.where(hit, w[k : k + 1, :].astype(F32), 0.0)
    before = jnp.where(
        lax.broadcasted_iota(jnp.int32, (tok, tok), 0)
        < lax.broadcasted_iota(jnp.int32, (tok, tok), 1),
        1.0,
        0.0,
    )
    rank = jnp.dot(member.astype(BF), before.astype(BF), preferred_element_type=F32)
    rank_s[...] = jnp.where(member > 0.0, rank + 1.0, 0.0)
    wt_s[...] = weight
    nth = lax.broadcasted_iota(jnp.int32, (CAP, tok), 0).astype(F32) + 1.0
    for d in range(4):
        for dx in range(4):
            e = expert_at(pos, d, dx)
            hit = nth == rank_s[pl.ds(e, 1), :]
            one = jnp.where(hit, 1.0, 0.0)
            s1[pl.ds((d * 4 + dx) * CAP, CAP), :] = one
            s2[pl.ds((dx * 4 + d) * CAP, CAP), :] = one
            sw2[pl.ds((dx * 4 + d) * CAP, CAP), :] = jnp.where(hit, wt_s[pl.ds(e, 1), :], 0.0)
    sel1 = s1[...].astype(BF)
    sel1_out[...] = sel1
    sel2_out[...] = s2[...].astype(BF)
    xv = jnp.dot(sel1, xin[...], preferred_element_type=F32).astype(BF)
    cv = jnp.dot(sw2[...].astype(BF), cot[...], preferred_element_type=F32).astype(BF)
    for i in range(4):
        rows[i][...] = xv[i * BLOCK : (i + 1) * BLOCK, :]
        ogs[i][...] = cv[i * BLOCK : (i + 1) * BLOCK, :]


SMEM = pl.BlockSpec(memory_space=pltpu.SMEM)
VMEM = pl.BlockSpec(memory_space=pltpu.VMEM)


def params(mib=48):
    return pltpu.CompilerParams(vmem_limit_bytes=mib * 1024 * 1024)


def cost(flops, nbytes):
    return pl.CostEstimate(flops=int(flops), bytes_accessed=int(nbytes), transcendentals=0)


def prep(pos, ids_t, w_t, xin, cot):
    tok, feat = xin.shape
    blk = jax.ShapeDtypeStruct((BLOCK, feat), BF)
    sel = jax.ShapeDtypeStruct((SLOTS, tok), BF)
    return pl.pallas_call(
        prep_kernel,
        out_shape=[blk] * 8 + [sel] * 2,
        in_specs=[SMEM, VMEM, VMEM, VMEM, VMEM],
        out_specs=[VMEM] * 10,
        scratch_shapes=[pltpu.VMEM((16, tok), F32)] * 2 + [pltpu.VMEM((SLOTS, tok), F32)] * 3,
        compiler_params=params(),
        cost_estimate=cost(4 * SLOTS * tok * feat, 4 * SLOTS * feat + 4 * tok * feat),
        name="prep",
    )(pos, ids_t, w_t, xin, cot)


def regroup_values(vals, j):
    return jnp.concatenate([v[j * CAP : (j + 1) * CAP, :] for v in vals], axis=0)


def regroup_kernel(*refs):
    vals = [r[...] for r in refs[:4]]
    for j in range(4):
        refs[4 + j][...] = regroup_values(vals, j)


def regroup(blocks, tile):
    width = blocks[0].shape[1]
    spec = pl.BlockSpec((BLOCK, tile), lambda i: (0, i))
    return pl.pallas_call(
        regroup_kernel,
        grid=(width // tile,),
        out_shape=[jax.ShapeDtypeStruct((BLOCK, width), BF)] * 4,
        in_specs=[spec] * 4,
        out_specs=[spec] * 4,
        compiler_params=params(),
        cost_estimate=cost(0, 4 * SLOTS * width),
        name="regroup",
    )(*blocks)


def assemble_kernel(*refs):
    x_out, og_out = refs[8], refs[9]
    x_out[...] = jnp.concatenate([r[...] for r in refs[:4]], axis=0)
    vals = [r[...] for r in refs[4:8]]
    og_out[...] = jnp.concatenate([regroup_values(vals, j) for j in range(4)], axis=0)


def assemble(xs, ogs):
    width = xs[0].shape[1]
    tile = 512
    spec = pl.BlockSpec((BLOCK, tile), lambda i: (0, i))
    out = pl.BlockSpec((SLOTS, tile), lambda i: (0, i))
    return pl.pallas_call(
        assemble_kernel,
        grid=(width // tile,),
        out_shape=[jax.ShapeDtypeStruct((SLOTS, width), BF)] * 2,
        in_specs=[spec] * 8,
        out_specs=[out] * 2,
        compiler_params=params(),
        cost_estimate=cost(0, 8 * SLOTS * width),
        name="assemble",
    )(*xs, *ogs)


def gather_w_kernel(pos, *refs):
    mine, other, out = refs[:4], refs[4], refs[5]
    sems = refs[6]
    zh, y, c = pos[2], pos[3], pos[4]
    copies = []
    for dc in range(2):
        for dy in range(4):
            for dzh in range(2):
                unit = (lax.rem(zh + dzh, 2) * 4 + lax.rem(y + dy, 4)) * 2 + lax.rem(c + dc, 2)
                src = mine[dy].at[dzh] if dc == 0 else other.at[dy, dzh]
                n = src.shape[0]
                copies.append(
                    pltpu.make_async_copy(
                        src,
                        out.at[pl.ds(pl.multiple_of(unit * n, 16), n), :],
                        sems.at[len(copies)],
                    )
                )
                copies[-1].start()
    for cp in copies:
        cp.wait()


def gather_w(pos, wd_t):
    part, hid = wd_t.shape
    other_z = send(wd_t, shift(dz=4))
    pair = jnp.stack([wd_t, other_z])
    got = [pair, send(pair, shift(dy=-1)), send(pair, shift(dy=2)), send(pair, shift(dy=1))]
    every = jnp.stack(got)
    flip = send(every, shift(dc=1))
    anys = pl.BlockSpec(memory_space=pl.ANY)
    return pl.pallas_call(
        gather_w_kernel,
        out_shape=jax.ShapeDtypeStruct((16 * part, hid), BF),
        in_specs=[SMEM] + [anys] * 5,
        out_specs=anys,
        scratch_shapes=[pltpu.SemaphoreType.DMA((16,))],
        compiler_params=params(8),
        cost_estimate=cost(0, 64 * part * hid),
        name="gather_w",
    )(pos, *got, flip)


def up_kernel(x, wg, wu, hidden, ca, cb):
    xv = x[...]
    gate = jnp.dot(xv, wg[0], preferred_element_type=F32)
    up = jnp.dot(xv, wu[0], preferred_element_type=F32)
    s = jax.nn.sigmoid(gate)
    silu = gate * s
    hidden[...] = (silu * up).astype(BF)
    ca[...] = up * s * (1.0 + gate * (1.0 - s))
    cb[...] = silu


def up_part(x, w):
    slots, feat = x.shape
    hid = w.shape[2] // 2
    tile = 256
    steps = hid // tile
    out = pl.BlockSpec((slots, tile), lambda i: (0, i))
    return pl.pallas_call(
        up_kernel,
        grid=(steps,),
        out_shape=[
            jax.ShapeDtypeStruct((slots, hid), BF),
            jax.ShapeDtypeStruct((slots, hid), F32),
            jax.ShapeDtypeStruct((slots, hid), F32),
        ],
        in_specs=[
            pl.BlockSpec((slots, feat), lambda i: (0, 0)),
            pl.BlockSpec((1, feat, tile), lambda i: (0, 0, i)),
            pl.BlockSpec((1, feat, tile), lambda i: (0, 0, i + steps)),
        ],
        out_specs=[out] * 3,
        compiler_params=params(),
        cost_estimate=cost(4 * slots * feat * hid, 4 * feat * hid + 2 * slots * feat),
        name="up_part",
    )(x, w, w)


def down_kernel(og, wd, hidden, ca, cb, pg, pu, dots):
    i = pl.program_id(0)
    hg = jnp.dot(og[...], wd[...], preferred_element_type=F32)
    pg[...] = (hg * ca[...]).astype(BF)
    pu[...] = (hg * cb[...]).astype(BF)
    part = jnp.sum(hg * hidden[...].astype(F32), axis=1, keepdims=True)

    @pl.when(i == 0)
    def _():
        dots[...] = jnp.zeros_like(dots)

    dots[...] += jnp.broadcast_to(part, dots.shape)


def down_part(og, wd, hidden, ca, cb):
    slots, feat = og.shape
    hid = hidden.shape[1]
    tile = 256
    col = pl.BlockSpec((slots, tile), lambda i: (0, i))
    return pl.pallas_call(
        down_kernel,
        grid=(hid // tile,),
        out_shape=[
            jax.ShapeDtypeStruct((slots, hid), BF),
            jax.ShapeDtypeStruct((slots, hid), BF),
            jax.ShapeDtypeStruct((slots, 128), F32),
        ],
        in_specs=[
            pl.BlockSpec((slots, feat), lambda i: (0, 0)),
            pl.BlockSpec((feat, tile), lambda i: (0, i)),
            col,
            col,
            col,
        ],
        out_specs=[col, col, pl.BlockSpec((slots, 128), lambda i: (0, 0))],
        compiler_params=params(),
        cost_estimate=cost(2 * slots * feat * hid, 2 * feat * hid + 2 * slots * feat),
        name="down_part",
    )(og, wd, hidden, ca, cb)


CONTRACT_LAST = (((1,), (1,)), ((), ()))
CONTRACT_FIRST = (((0,), (0,)), ((), ()))


def row_kernel(tile, regrouped, pg, pu, w, *refs):
    i = pl.program_id(0)
    hid = pg.shape[1]
    g = lax.dot_general(pg[...], w[0, :, :hid], CONTRACT_LAST, preferred_element_type=F32)
    g = g + lax.dot_general(pu[...], w[0, :, hid:], CONTRACT_LAST, preferred_element_type=F32)
    g = g.astype(BF)
    at = pl.ds(pl.multiple_of(i * tile, tile), tile)
    vals = [g[j * BLOCK : (j + 1) * BLOCK, :] for j in range(4)]
    if not regrouped:
        for j in range(4):
            refs[j][:, at] = vals[j]
        return
    dots, outs = refs[0], refs[1:]
    for j in range(4):
        outs[j][:, at] = regroup_values(vals, j)

    @pl.when(i == 0)
    def _():
        dv = dots[...]
        hi = dv.astype(BF)
        lo = (dv - hi.astype(F32)).astype(BF)
        lane = lax.broadcasted_iota(jnp.int32, dv.shape, 1)
        both = jnp.where(lane == 0, hi.astype(F32), lo.astype(F32)).astype(BF)
        cols = outs[0].shape[1] - 128
        parts = [both[j * BLOCK : (j + 1) * BLOCK, :] for j in range(4)]
        for j in range(4):
            outs[j][:, cols:] = regroup_values(parts, j)


def row_part(pg, pu, w, first, count, dots=None):
    slots, hid = pg.shape
    tile = 256
    start = first // tile
    whole = lambda shape: pl.BlockSpec(shape, lambda i: (0, 0))
    width = count + (0 if dots is None else 128)
    extra = [] if dots is None else [dots]
    return pl.pallas_call(
        functools.partial(row_kernel, tile, dots is not None),
        grid=(count // tile,),
        out_shape=[jax.ShapeDtypeStruct((BLOCK, width), BF)] * 4,
        in_specs=[
            whole((slots, hid)),
            whole((slots, hid)),
            pl.BlockSpec((1, tile, 2 * hid), lambda i: (0, i + start, 0)),
        ]
        + [whole((slots, 128)) for _ in extra],
        out_specs=[whole((BLOCK, width))] * 4,
        compiler_params=params(),
        cost_estimate=cost(4 * slots * count * hid, 4 * count * hid + 6 * slots * hid),
        name="row_part",
    )(pg, pu, w, *extra)


def grad_kernel(part, pos, left, right, mine, other):
    b = pl.program_id(0)
    res = lax.dot_general(left[...], right[...], CONTRACT_FIRST, preferred_element_type=F32)
    res = res.astype(BF)
    for j in range(2):
        at = pos[5 + b * 2 + j]
        p0 = res[(2 * j) * part : (2 * j + 1) * part, :]
        p1 = res[(2 * j + 1) * part : (2 * j + 2) * part, :]

        @pl.when(pos[4] == 0)
        def _():
            mine[at] = p0
            other[at] = p1

        @pl.when(pos[4] == 1)
        def _():
            mine[at] = p1
            other[at] = p0


def grad_part(pos, left, right):
    slots, feat = left.shape
    cols = right.shape[1]
    part = feat // 16
    out = jax.ShapeDtypeStruct((8, part, cols), BF)
    whole = pl.BlockSpec((8, part, cols), lambda i: (0, 0, 0))
    return pl.pallas_call(
        functools.partial(grad_kernel, part),
        grid=(4,),
        out_shape=[out] * 2,
        in_specs=[
            SMEM,
            pl.BlockSpec((slots, 4 * part), lambda i: (0, i)),
            pl.BlockSpec((slots, cols), lambda i: (0, 0)),
        ],
        out_specs=[whole] * 2,
        compiler_params=params(),
        cost_estimate=cost(2 * slots * feat * cols, 2 * feat * cols + 2 * slots * feat),
        name="grad_part",
    )(pos, left, right)


def plus(*vals):
    return sum(v.astype(F32) for v in vals)


def reduce_chunk(mine, other):
    got = send(other, shift(dc=1))
    add = lambda a, b: plus(mine[a:b], got[a:b]).astype(BF)
    up1 = send(add(0, 2), shift(dy=1))
    dn1 = send(add(2, 4), shift(dy=-1))
    up2 = send(plus(mine[4], got[4], up1[0]).astype(BF), shift(dy=1))
    dn2 = send(plus(mine[5], got[5], dn1[0]).astype(BF), shift(dy=-1))
    far = send(plus(mine[7], got[7], up1[1], dn2).astype(BF), shift(dz=4))
    return plus(mine[6], got[6], dn1[1], up2, far)


def final_kernel(pos, ids, w, sel1, sel2, *refs):
    back_a, back_b, grad, gate = refs[:4], refs[4:8], refs[8], refs[9]
    half = back_a[0].shape[1]
    feat = grad.shape[1]
    acc_a = jnp.zeros((grad.shape[0], half), F32)
    acc_b = jnp.zeros((grad.shape[0], feat - half), F32)
    s1, s2 = sel1[...].astype(F32), sel2[...].astype(F32)
    gates = [jnp.zeros((1, grad.shape[0]), F32) for _ in range(3)]
    for j in range(4):
        p1 = s1[j * BLOCK : (j + 1) * BLOCK, :]
        p2 = s2[j * BLOCK : (j + 1) * BLOCK, :]
        acc_a += lax.dot_general(
            p1.astype(BF), back_a[j][...], CONTRACT_FIRST, preferred_element_type=F32
        )
        acc_b += lax.dot_general(
            p2.astype(BF), back_b[j][:, : feat - half], CONTRACT_FIRST, preferred_element_type=F32
        )
        tail = back_b[j][:, feat - half :].astype(F32)
        dv = tail[:, 0:1] + tail[:, 1:2]
        found = p2 * dv
        for d in range(4):
            val = jnp.sum(found[d * CAP : (d + 1) * CAP, :], axis=0, keepdims=True)
            e = expert_at(pos, d, j)
            for k in range(3):
                gates[k] += jnp.where(ids[k : k + 1, :] == e, val, 0.0)
    grad[:, :half] = acc_a.astype(BF)
    grad[:, half:] = acc_b.astype(BF)
    for k in range(3):
        gate[k : k + 1, :] = (gates[k] / w[k : k + 1, :].astype(F32)).astype(BF)


def final(pos, ids_t, w_t, sel1, sel2, back_a, back_b, feat):
    tok = ids_t.shape[1]
    return pl.pallas_call(
        final_kernel,
        out_shape=[jax.ShapeDtypeStruct((tok, feat), BF), jax.ShapeDtypeStruct((3, tok), BF)],
        in_specs=[SMEM] + [VMEM] * 12,
        out_specs=[VMEM] * 2,
        compiler_params=params(),
        cost_estimate=cost(2 * SLOTS * tok * feat, 2 * SLOTS * feat + 2 * tok * feat),
        name="final",
    )(pos, ids_t, w_t, sel1, sel2, *back_a, *back_b)


def on_device(layer_inputs, cotangent, expert_ids, route_weights, w_gate_up, w_down):
    feat = layer_inputs.shape[1]
    zh, y, c, x, zl = (lax.axis_index(a) for a in AXES)
    places = jnp.zeros((8,), jnp.int32)
    unit = jnp.arange(8, dtype=jnp.int32)
    rel = ((unit % 4 - y) % 4) * 2 + (unit // 4 + zh) % 2
    for (dy, dzh), at in PLACE.items():
        places = jnp.where(rel == dy * 2 + dzh, at, places)
    pos = jnp.concatenate([jnp.stack([x, zl, zh, y, c]).astype(jnp.int32), places])
    ids_t, w_t = expert_ids.T, route_weights.T

    made = prep(pos, ids_t, w_t, layer_inputs, cotangent)
    rows, ogs, sel1, sel2 = made[:4], made[4:8], made[8], made[9]
    z_moves = [z_window(d) for d in (1, 2, 3)]
    x_moves = [shift(dx=d) for d in (1, 2, 3)]
    over = lambda blocks, moves: [blocks[0]] + [send(b, m) for b, m in zip(blocks[1:], moves)]
    home = lambda blocks, moves: over(blocks, [back(m) for m in moves])
    rows = regroup(over(rows, z_moves), 512)
    ogs = regroup(over(ogs, x_moves), 512)
    wd_all = gather_w(pos, w_down[0].T)
    xs, og = assemble(over(rows, x_moves), over(ogs, z_moves))

    hidden, ca, cb = up_part(xs, w_gate_up)
    down_mine, down_other = grad_part(pos, og, hidden)
    pg, pu, dots = down_part(og, wd_all, hidden, ca, cb)
    gate_mine, gate_other = grad_part(pos, xs, pg)
    half = feat // 2
    rows_a = row_part(pg, pu, w_gate_up, 0, half)
    up_mine, up_other = grad_part(pos, xs, pu)
    rows_b = row_part(pg, pu, w_gate_up, half, half, dots)

    down_grad = reduce_chunk(down_mine, down_other).astype(BF)
    gate_sum = reduce_chunk(gate_mine, gate_other)
    up_sum = reduce_chunk(up_mine, up_other)

    back_a = home(regroup(home(rows_a, x_moves), half // 2), z_moves)
    back_b = home(regroup(home(rows_b, z_moves), (half + 128) // 11), x_moves)
    input_grad, gate_grad = final(pos, ids_t, w_t, sel1, sel2, back_a, back_b, feat)
    gu_grad = jnp.concatenate([gate_sum, up_sum], axis=1).astype(BF)
    return (input_grad, gate_grad.T, gu_grad[None], down_grad.T[None])


def solution(mesh):
    grid = Mesh(mesh.devices.reshape(SIZES), AXES)
    dp, ex = AXES[:3], AXES[3:]
    return jax.shard_map(
        on_device,
        mesh=grid,
        in_specs=(
            P(AXES, None),
            P(AXES, None),
            P(AXES, None),
            P(AXES, None),
            P(ex, None, None),
            P(ex, None, dp),
        ),
        out_specs=(
            P(AXES, None),
            P(AXES, None),
            P(ex, dp, None),
            P(ex, None, dp),
        ),
        check_vma=False,
    )
```

```python
import functools

import jax
import jax.numpy as jnp
import numpy as np
from jax import lax
from jax.experimental import pallas as pl
from jax.experimental.pallas import tpu as pltpu
from jax.sharding import Mesh
from jax.sharding import PartitionSpec as P

AXES = ("zh", "y", "c", "x", "zl")
SIZES = (2, 4, 2, 4, 4)
CAP = 26
BLOCK = 4 * CAP
SLOTS = 16 * CAP
BF = jnp.bfloat16
F32 = jnp.float32
PLACE = {(2, 0): 0, (1, 1): 1, (2, 1): 2, (3, 0): 3, (1, 0): 4, (3, 1): 5, (0, 0): 6, (0, 1): 7}


def pairs_of(move):
    out = []
    for i in range(int(np.prod(SIZES))):
        zh, y, c, x, zl = (int(v) for v in np.unravel_index(i, SIZES))
        z, y, c, x = move(zh * 4 + zl, y, c, x)
        z, y, c, x = z % 8, y % 4, c % 2, x % 4
        out.append((i, int(np.ravel_multi_index((z // 4, y, c, x, z % 4), SIZES))))
    return out


def shift(dz=0, dy=0, dc=0, dx=0):
    return pairs_of(lambda z, y, c, x: (z + dz, y + dy, c + dc, x + dx))


def z_window(d):
    if d == 2:
        return pairs_of(lambda z, y, c, x: (z + 2 - 4 * (z % 2), y, c, x))
    return shift(dz=1 if d == 1 else -1)


def back(pairs):
    return [(b, a) for a, b in pairs]


def send(v, pairs):
    return lax.ppermute(v, AXES, pairs)


def expert_at(pos, d, dx):
    return lax.rem(pos[0] + dx, 4) * 4 + lax.rem(pos[1] + d, 4)


def prep_kernel(pos, ids, w, xin, cot, *refs):
    rows, ogs, sel_out = refs[:4], refs[4:8], refs[8]
    rank_s, wt_s, s1, s2, sw2 = refs[9:]
    tok = ids.shape[1]
    eid = lax.broadcasted_iota(jnp.int32, (16, tok), 0)
    member = jnp.zeros((16, tok), F32)
    weight = jnp.zeros((16, tok), F32)
    for k in range(3):
        hit = eid == ids[k : k + 1, :]
        member = member + jnp.where(hit, 1.0, 0.0)
        weight = weight + jnp.where(hit, w[k : k + 1, :].astype(F32), 0.0)
    before = jnp.where(
        lax.broadcasted_iota(jnp.int32, (tok, tok), 0)
        < lax.broadcasted_iota(jnp.int32, (tok, tok), 1),
        1.0,
        0.0,
    )
    rank = jnp.dot(member.astype(BF), before.astype(BF), preferred_element_type=F32)
    rank_s[...] = jnp.where(member > 0.0, rank + 1.0, 0.0)
    wt_s[...] = weight
    nth = lax.broadcasted_iota(jnp.int32, (CAP, tok), 0).astype(F32) + 1.0
    for d in range(4):
        for dx in range(4):
            e = expert_at(pos, d, dx)
            hit = nth == rank_s[pl.ds(e, 1), :]
            one = jnp.where(hit, 1.0, 0.0)
            s1[pl.ds((d * 4 + dx) * CAP, CAP), :] = one
            s2[pl.ds((dx * 4 + d) * CAP, CAP), :] = one
            sw2[pl.ds((dx * 4 + d) * CAP, CAP), :] = jnp.where(hit, wt_s[pl.ds(e, 1), :], 0.0)
    sel1 = s1[...].astype(BF)
    sel_out[...] = s2[...].astype(BF)
    xv = jnp.dot(sel1, xin[...], preferred_element_type=F32).astype(BF)
    cv = jnp.dot(sw2[...].astype(BF), cot[...], preferred_element_type=F32).astype(BF)
    for i in range(4):
        rows[i][...] = xv[i * BLOCK : (i + 1) * BLOCK, :]
        ogs[i][...] = cv[i * BLOCK : (i + 1) * BLOCK, :]


SMEM = pl.BlockSpec(memory_space=pltpu.SMEM)
VMEM = pl.BlockSpec(memory_space=pltpu.VMEM)


def params(mib=16):
    return pltpu.CompilerParams(vmem_limit_bytes=mib * 1024 * 1024)


def call(kernel, args, in_specs, out_shape, out_specs, deps=(), **kw):
    n, m = len(args), len(deps)

    def body(*refs):
        kernel(*refs[:n], *refs[n + m :])

    specs = list(in_specs) + [pl.BlockSpec(memory_space=pl.ANY)] * m
    kw.setdefault("compiler_params", params())
    return pl.pallas_call(body, out_shape=out_shape, in_specs=specs, out_specs=out_specs, **kw)(
        *args, *deps
    )


def cost(flops, nbytes):
    return pl.CostEstimate(flops=int(flops) // 64, bytes_accessed=int(nbytes) // 64, transcendentals=0)


def prep(pos, ids_t, w_t, xin, cot, deps):
    tok, feat = xin.shape
    blk = jax.ShapeDtypeStruct((BLOCK, feat), BF)
    sel = jax.ShapeDtypeStruct((SLOTS, tok), BF)
    return call(
        prep_kernel,
        (pos, ids_t, w_t, xin, cot),
        [SMEM, VMEM, VMEM, VMEM, VMEM],
        [blk] * 8 + [sel],
        [VMEM] * 9,
        deps,
        scratch_shapes=[pltpu.VMEM((16, tok), F32)] * 2 + [pltpu.VMEM((SLOTS, tok), F32)] * 3,
        compiler_params=params(28),
        cost_estimate=cost(4 * SLOTS * tok * feat, 4 * SLOTS * feat + 4 * tok * feat),
        name="prep",
    )


def regroup_values(vals, j):
    return jnp.concatenate([v[j * CAP : (j + 1) * CAP, :] for v in vals], axis=0)


def regroup_kernel(*refs):
    vals = [r[...] for r in refs[:4]]
    for j in range(4):
        refs[4 + j][...] = regroup_values(vals, j)


def regroup(blocks, tile, deps=()):
    width = blocks[0].shape[1]
    spec = pl.BlockSpec((BLOCK, tile), lambda i: (0, i))
    return call(
        regroup_kernel,
        blocks,
        [spec] * 4,
        [jax.ShapeDtypeStruct((BLOCK, width), BF)] * 4,
        [spec] * 4,
        deps,
        grid=(width // tile,),
        cost_estimate=cost(0, 4 * SLOTS * width),
        name="regroup",
    )


def copies_kernel(v, out):
    for k in range(4):
        out[k] = v[...]


def four_copies(v, deps):
    return call(
        copies_kernel,
        (v,),
        [VMEM],
        jax.ShapeDtypeStruct((4,) + v.shape, BF),
        VMEM,
        deps,
        cost_estimate=cost(0, 10 * v.size),
        name="four_copies",
    )


def stack_kernel(pos, *refs):
    vals = [r[...] for r in refs[:4]]
    for j in range(4):
        refs[4][lax.rem(pos[0] - j + 4, 4)] = regroup_values(vals, j)


def regroup_stacked(pos, blocks, tile, deps):
    width = blocks[0].shape[1]
    return call(
        stack_kernel,
        (pos, *blocks),
        [SMEM] + [pl.BlockSpec((BLOCK, tile), lambda i: (0, i))] * 4,
        jax.ShapeDtypeStruct((4, BLOCK, width), BF),
        pl.BlockSpec((4, BLOCK, tile), lambda i: (0, 0, i)),
        deps,
        grid=(width // tile,),
        cost_estimate=cost(0, 4 * SLOTS * width),
        name="regroup",
    )


def assemble_kernel(*refs):
    x_out, og_out = refs[8], refs[9]
    x_out[...] = jnp.concatenate([r[...] for r in refs[:4]], axis=0)
    vals = [r[...] for r in refs[4:8]]
    og_out[...] = jnp.concatenate([regroup_values(vals, j) for j in range(4)], axis=0)


def assemble(xs, ogs, deps):
    width = xs[0].shape[1]
    tile = 512
    spec = pl.BlockSpec((BLOCK, tile), lambda i: (0, i))
    out = pl.BlockSpec((SLOTS, tile), lambda i: (0, i))
    return call(
        assemble_kernel,
        (*xs, *ogs),
        [spec] * 8,
        [jax.ShapeDtypeStruct((SLOTS, width), BF)] * 2,
        [out] * 2,
        deps,
        grid=(width // tile,),
        cost_estimate=cost(0, 8 * SLOTS * width),
        name="assemble",
    )


def hold(v, deps):
    anys = pl.BlockSpec(memory_space=pl.ANY)
    return call(
        lambda v_ref, out_ref: None,
        (v,),
        [anys],
        jax.ShapeDtypeStruct(v.shape, v.dtype),
        anys,
        deps,
        input_output_aliases={0: 0},
        name="hold",
    )


def up_kernel(x, wg, wu, hidden, ca, cb):
    xv = x[...]
    gate = jnp.dot(xv, wg[0], preferred_element_type=F32)
    up = jnp.dot(xv, wu[0], preferred_element_type=F32)
    s = jax.nn.sigmoid(gate)
    silu = gate * s
    hidden[...] = (silu * up).astype(BF)
    ca[...] = up * s * (1.0 + gate * (1.0 - s))
    cb[...] = silu


def up_part(x, w):
    slots, feat = x.shape
    hid = w.shape[2] // 2
    tile = 256
    steps = hid // tile
    out = pl.BlockSpec((slots, tile), lambda i: (0, i))
    return pl.pallas_call(
        up_kernel,
        grid=(steps,),
        out_shape=[
            jax.ShapeDtypeStruct((slots, hid), BF),
            jax.ShapeDtypeStruct((slots, hid), F32),
            jax.ShapeDtypeStruct((slots, hid), F32),
        ],
        in_specs=[
            pl.BlockSpec((slots, feat), lambda i: (0, 0)),
            pl.BlockSpec((1, feat, tile), lambda i: (0, 0, i)),
            pl.BlockSpec((1, feat, tile), lambda i: (0, 0, i + steps)),
        ],
        out_specs=[out] * 3,
        compiler_params=params(46),
        cost_estimate=cost(4 * slots * feat * hid, 4 * feat * hid + 2 * slots * feat),
        name="up_part",
    )(x, w, w)


def down_kernel(part, *refs):
    pos, og, w_own, w_other, hidden, ca, cb = refs[:7]
    pg, pu, dots, wbuf, acc, hv, av, bv, sems = refs[-9:]
    b = pl.program_id(0)
    moves = [
        pltpu.make_async_copy(src, dst, sems.at[k])
        for k, (src, dst) in enumerate(((hidden, hv), (ca, av), (cb, bv)))
    ]

    @pl.when(b == 0)
    def _():
        for m in moves:
            m.start()
        acc[...] = jnp.zeros_like(acc)

    c = pos[4]
    for j in range(2):
        own = pl.multiple_of((2 * j + c) * part, 32)
        other = pl.multiple_of((2 * j + 1 - c) * part, 32)
        wbuf[pl.ds(own, part), :] = w_own[j, 0]
        wbuf[pl.ds(other, part), :] = w_other[j, 0]
    acc[...] += jnp.dot(og[...], wbuf[...], preferred_element_type=F32)

    @pl.when(b == pl.num_programs(0) - 1)
    def _():
        for m in moves:
            m.wait()
        hg = acc[...]
        pg[...] = (hg * av[...]).astype(BF)
        pu[...] = (hg * bv[...]).astype(BF)
        part_dots = jnp.sum(hg * hv[...].astype(F32), axis=1, keepdims=True)
        dots[...] = jnp.broadcast_to(part_dots, dots.shape)


def down_part(pos, og, w_own, w_other, hidden, ca, cb, deps):
    slots, feat = og.shape
    hid = hidden.shape[1]
    part = w_own.shape[2]
    w_spec = pl.BlockSpec(
        (2, 1, part, hid), lambda b, p: (lax.rem(b, 2), lax.div(b, 2), 0, 0)
    )
    anys = pl.BlockSpec(memory_space=pl.ANY)
    whole = lambda *shape: pl.BlockSpec(shape, lambda b, p: (0,) * len(shape))
    return pl.pallas_call(
        functools.partial(down_kernel, part),
        out_shape=[
            jax.ShapeDtypeStruct((slots, hid), BF),
            jax.ShapeDtypeStruct((slots, hid), BF),
            jax.ShapeDtypeStruct((slots, 128), F32),
        ],
        grid_spec=pltpu.PrefetchScalarGridSpec(
            num_scalar_prefetch=1,
            grid=(4,),
            in_specs=[pl.BlockSpec((slots, 4 * part), lambda b, p: (0, b)), w_spec, w_spec]
            + [anys] * (3 + len(deps)),
            out_specs=[whole(slots, hid), whole(slots, hid), whole(slots, 128)],
            scratch_shapes=[
                pltpu.VMEM((4 * part, hid), BF),
                pltpu.VMEM((slots, hid), F32),
                pltpu.VMEM((slots, hid), BF),
                pltpu.VMEM((slots, hid), F32),
                pltpu.VMEM((slots, hid), F32),
                pltpu.SemaphoreType.DMA((3,)),
            ],
        ),
        compiler_params=params(28),
        cost_estimate=cost(2 * slots * feat * hid, 2 * feat * hid + 2 * slots * feat),
        name="down_part",
    )(pos, og, w_own, w_other, hidden, ca, cb, *deps)


CONTRACT_LAST = (((1,), (1,)), ((), ()))
CONTRACT_FIRST = (((0,), (0,)), ((), ()))


def row_kernel(tile, pg, pu, w, dots, *outs):
    i = pl.program_id(0)
    hid = pg.shape[1]
    g = lax.dot_general(pg[...], w[0, :, :hid], CONTRACT_LAST, preferred_element_type=F32)
    g = g + lax.dot_general(pu[...], w[0, :, hid:], CONTRACT_LAST, preferred_element_type=F32)
    g = g.astype(BF)
    at = pl.ds(pl.multiple_of(i * tile, tile), tile)
    vals = [g[j * BLOCK : (j + 1) * BLOCK, :] for j in range(4)]
    for j in range(4):
        outs[j][:, at] = regroup_values(vals, j)

    @pl.when(i == 0)
    def _():
        dv = dots[...]
        hi = dv.astype(BF)
        lo = (dv - hi.astype(F32)).astype(BF)
        lane = lax.broadcasted_iota(jnp.int32, dv.shape, 1)
        both = jnp.where(lane == 0, hi.astype(F32), lo.astype(F32)).astype(BF)
        cols = outs[0].shape[1] - 128
        parts = [both[j * BLOCK : (j + 1) * BLOCK, :] for j in range(4)]
        for j in range(4):
            outs[j][:, cols:] = regroup_values(parts, j)


def row_part(pg, pu, w, dots, deps):
    slots, hid = pg.shape
    feat = w.shape[1]
    tile = 256
    whole = lambda *shape: pl.BlockSpec(shape, lambda i: (0,) * len(shape))
    return call(
        functools.partial(row_kernel, tile),
        (pg, pu, w, dots),
        [
            whole(slots, hid),
            whole(slots, hid),
            pl.BlockSpec((1, tile, 2 * hid), lambda i: (0, i, 0)),
            whole(slots, 128),
        ],
        [jax.ShapeDtypeStruct((BLOCK, feat + 128), BF)] * 4,
        [whole(BLOCK, feat + 128)] * 4,
        deps,
        grid=(feat // tile,),
        compiler_params=params(24),
        cost_estimate=cost(4 * slots * feat * hid, 4 * feat * hid + 6 * slots * hid),
        name="row_part",
    )


def grad_kernel(part, pos, left, *refs):
    rights, mine, other, buf, sems = refs[:-4], refs[-4], refs[-3], refs[-2], refs[-1]
    b = pl.program_id(0)
    slot = lax.rem(b, 2)

    def finish(which):
        for u in range(4):
            pltpu.make_async_copy(buf.at[which, u], mine.at[0], sems.at[which, u]).wait()

    @pl.when(b >= 2)
    def _():
        finish(slot)

    lv = left[...].T
    for k, right in enumerate(rights):
        res = jnp.dot(lv, right[...], preferred_element_type=F32).astype(BF)
        cols = slice(k * res.shape[1], (k + 1) * res.shape[1])
        for u in range(4):
            buf[slot, u, :, cols] = res[u * part : (u + 1) * part, :]

    def out(c):
        for u in range(4):
            to = mine if u % 2 == c else other
            at = pos[5 + b * 2 + u // 2]
            pltpu.make_async_copy(buf.at[slot, u], to.at[at], sems.at[slot, u]).start()

    pl.when(pos[4] == 0)(lambda: out(0))
    pl.when(pos[4] == 1)(lambda: out(1))

    @pl.when(b == pl.num_programs(0) - 1)
    def _():
        finish(1 - slot)
        finish(slot)


def grad_part(pos, left, rights, deps=()):
    slots, feat = left.shape
    cols = sum(r.shape[1] for r in rights)
    part = feat // 16
    return call(
        functools.partial(grad_kernel, part),
        (pos, left, *rights),
        [SMEM, pl.BlockSpec((slots, 4 * part), lambda i: (0, i))]
        + [pl.BlockSpec(r.shape, lambda i: (0, 0)) for r in rights],
        [jax.ShapeDtypeStruct((8, part, cols), BF)] * 2,
        [pl.BlockSpec(memory_space=pl.ANY)] * 2,
        deps,
        grid=(4,),
        scratch_shapes=[pltpu.VMEM((2, 4, part, cols), BF), pltpu.SemaphoreType.DMA((2, 4))],
        compiler_params=params(24),
        cost_estimate=cost(2 * slots * feat * cols, 2 * feat * cols + 2 * slots * feat),
        name="grad_part",
    )


def plus(*vals):
    return sum(v.astype(F32) for v in vals)


def first_kernel(mine, got, up, down):
    total = plus(mine[...], got[...]).astype(BF)
    up[...] = total[:2]
    down[...] = total[2:]


def second_kernel(mine, got, up1, dn1, up, down):
    total = plus(mine[...], got[...])
    up[...] = plus(total[0], up1[0]).astype(BF)
    down[...] = plus(total[1], dn1[0]).astype(BF)


def far_kernel(mine, got, up1, dn1, up2, dn2, out, kept):
    out[...] = plus(mine[1], got[1], up1[0], dn2[...]).astype(BF)
    kept[...] = plus(mine[0], got[0], dn1[0], up2[...])


def last_kernel(kept, far, out):
    out[...] = plus(kept[...], far[...]).astype(BF)


def pieces(shape, count, at, tile):
    return pl.BlockSpec((count,) + shape[1:-1] + (tile,), lambda i: (at, 0, i))


def sums(kernel, args, specs, outs, deps, name):
    tile = 384
    cols = args[0].shape[-1]
    flat = pl.BlockSpec((args[0].shape[-2], tile), lambda i: (0, i))
    nbytes = sum(2 * (sp[0] if sp else 1) * args[0].shape[-2] * cols for sp in specs)
    return call(
        kernel,
        args,
        [flat if sp is None else pieces(a.shape, sp[0], sp[1], tile) for a, sp in zip(args, specs)],
        outs,
        [flat if len(o.shape) == 2 else pieces(o.shape, o.shape[0], 0, tile) for o in outs],
        deps,
        grid=(cols // tile,),
        cost_estimate=cost(0, 2 * nbytes),
        name=name,
    )


def shape_of(a, count=None):
    return jax.ShapeDtypeStruct(((count,) if count else ()) + a.shape[1:], BF)


def first_sum(mine, got, deps):
    args, outs = (mine, got), [shape_of(mine, 2)] * 2
    up, down = sums(first_kernel, args, [(4, 0)] * 2, outs, deps, "first_sum")
    return send(up, shift(dy=1)), send(down, shift(dy=-1)), [up]


def second_sum(mine, got, up1, dn1, deps):
    args, outs = (mine, got, up1, dn1), [shape_of(mine)] * 2
    specs = [(2, 2), (2, 2), (1, 0), (1, 0)]
    up, down = sums(second_kernel, args, specs, outs, deps, "second_sum")
    return send(up, shift(dy=1)), send(down, shift(dy=-1)), [up]


def far_sum(mine, got, up1, dn1, up2, dn2, deps):
    args = (mine, got, up1, dn1, up2, dn2)
    outs = [shape_of(mine), jax.ShapeDtypeStruct(mine.shape[1:], F32)]
    specs = [(2, 3), (2, 3), (1, 1), (1, 1), None, None]
    out, kept = sums(far_kernel, args, specs, outs, deps, "far_sum")
    return send(out, shift(dz=4)), kept, [out]


def last_sum(kept, far, deps):
    (out,) = sums(last_kernel, (kept, far), [None] * 2, [shape_of(kept[None])], deps, "last_sum")
    return out


def final_kernel(pos, ids, w, sel, back, grad, gate):
    feat = grad.shape[1]
    acc = jnp.zeros(grad.shape, F32)
    sv = sel[...].astype(F32)
    gates = [jnp.zeros((1, grad.shape[0]), F32) for _ in range(3)]
    for j in range(4):
        at = lax.rem(pos[0] + j, 4)
        part = sv[j * BLOCK : (j + 1) * BLOCK, :]
        acc += lax.dot_general(
            part.astype(BF), back[at, :, :feat], CONTRACT_FIRST, preferred_element_type=F32
        )
        tail = back[at, :, feat:].astype(F32)
        found = part * (tail[:, 0:1] + tail[:, 1:2])
        for d in range(4):
            val = jnp.sum(found[d * CAP : (d + 1) * CAP, :], axis=0, keepdims=True)
            e = expert_at(pos, d, j)
            for k in range(3):
                gates[k] += jnp.where(ids[k : k + 1, :] == e, val, 0.0)
    grad[...] = acc.astype(BF)
    for k in range(3):
        gate[k : k + 1, :] = (gates[k] / w[k : k + 1, :].astype(F32)).astype(BF)


def final(pos, ids_t, w_t, sel, back, feat, deps):
    tok = ids_t.shape[1]
    return call(
        final_kernel,
        (pos, ids_t, w_t, sel, back),
        [SMEM] + [VMEM] * 4,
        [jax.ShapeDtypeStruct((tok, feat), BF), jax.ShapeDtypeStruct((3, tok), BF)],
        [VMEM] * 2,
        deps,
        cost_estimate=cost(2 * SLOTS * tok * feat, 2 * SLOTS * feat + 2 * tok * feat),
        name="final",
    )


def on_device(layer_inputs, cotangent, expert_ids, route_weights, w_gate_up, w_down):
    feat = layer_inputs.shape[1]
    zh, y, c, x, zl = (lax.axis_index(a) for a in AXES)
    places = jnp.zeros((8,), jnp.int32)
    unit = jnp.arange(8, dtype=jnp.int32)
    rel = ((unit % 4 - y) % 4) * 2 + (unit // 4 + zh) % 2
    for (dy, dzh), at in PLACE.items():
        places = jnp.where(rel == dy * 2 + dzh, at, places)
    pos = jnp.concatenate([jnp.stack([x, zl, zh, y, c]).astype(jnp.int32), places])
    ids_t, w_t = expert_ids.T, route_weights.T

    wd = w_down[0].T
    wd_two = jnp.stack([wd, wd])
    wd_zh = lax.all_to_all(wd_two, "zh", 0, 0, tiled=True)
    made = prep(pos, ids_t, w_t, layer_inputs, cotangent, [wd_two])
    rows, ogs, sel = made[:4], made[4:8], made[8]
    z_moves = [z_window(d) for d in (1, 2, 3)]
    x_moves = [shift(dx=d) for d in (1, 2, 3)]
    over = lambda blocks, moves: [blocks[0]] + [send(b, m) for b, m in zip(blocks[1:], moves)]
    home = lambda blocks, moves: over(blocks, [back(m) for m in moves])
    flip = lambda v: send(v, shift(dc=1))
    rows = over(rows, z_moves)
    pairs = four_copies(wd_zh, [rows[1]])
    rows = regroup(rows, 512, [pairs])
    wd_own = lax.all_to_all(pairs, "y", 0, 0, tiled=True)
    ogs = regroup(over(ogs, x_moves), 512, [rows[0]])
    xs, og = assemble(over(rows, x_moves), over(ogs, z_moves), [])
    wd_own = hold(wd_own, [xs])
    wd_other = flip(wd_own)

    hidden, ca, cb = up_part(xs, w_gate_up)
    pg, pu, dots = down_part(pos, og, wd_own, wd_other, hidden, ca, cb, [])
    g_own, other = grad_part(pos, xs, [pg, pu])
    g_got = flip(other)
    d_own, other = grad_part(pos, og, [hidden], [g_own])
    d_got = flip(other)
    g_up1, g_dn1, dep = first_sum(g_own, g_got, [d_own])
    d_up1, d_dn1, dep = first_sum(d_own, d_got, dep)
    row_grads = row_part(pg, pu, w_gate_up, dots, dep)
    g_up2, g_dn2, dep = second_sum(g_own, g_got, g_up1, g_dn1, [row_grads[0]])
    g_far, g_kept, dep = far_sum(g_own, g_got, g_up1, g_dn1, g_up2, g_dn2, dep)
    back_rows = regroup_stacked(pos, home(row_grads, z_moves), (feat + 128) // 3, dep)
    back_rows_x = lax.all_to_all(back_rows, "x", 0, 0, tiled=True)
    d_up2, d_dn2, dep = second_sum(d_own, d_got, d_up1, d_dn1, [back_rows])
    gu_grad = last_sum(g_kept, g_far, dep)
    d_far, d_kept, dep = far_sum(d_own, d_got, d_up1, d_dn1, d_up2, d_dn2, [gu_grad])
    input_grad, gate_grad = final(pos, ids_t, w_t, sel, back_rows_x, feat, dep)
    down_grad = last_sum(d_kept, d_far, [input_grad])
    return (input_grad, gate_grad.T, gu_grad[None], down_grad.T[None])


def solution(mesh):
    grid = Mesh(mesh.devices.reshape(SIZES), AXES)
    dp, ex = AXES[:3], AXES[3:]
    return jax.shard_map(
        on_device,
        mesh=grid,
        in_specs=(
            P(AXES, None),
            P(AXES, None),
            P(AXES, None),
            P(AXES, None),
            P(ex, None, None),
            P(ex, None, dp),
        ),
        out_specs=(
            P(AXES, None),
            P(AXES, None),
            P(ex, dp, None),
            P(ex, None, dp),
        ),
        check_vma=False,
    )
```

```python
import functools

import jax
import jax.numpy as jnp
import numpy as np
from jax import lax
from jax.experimental import pallas as pl
from jax.experimental.pallas import tpu as pltpu
from jax.sharding import Mesh
from jax.sharding import PartitionSpec as P

AXES = ("zh", "y", "c", "x", "zl")
SIZES = (2, 4, 2, 4, 4)
CAP = 26
BLOCK = 4 * CAP
SLOTS = 16 * CAP
BF = jnp.bfloat16
F32 = jnp.float32
PLACE = {(2, 0): 0, (1, 1): 1, (2, 1): 2, (3, 0): 3, (1, 0): 4, (3, 1): 5, (0, 0): 6, (0, 1): 7}


def pairs_of(move):
    out = []
    for i in range(int(np.prod(SIZES))):
        zh, y, c, x, zl = (int(v) for v in np.unravel_index(i, SIZES))
        z, y, c, x = move(zh * 4 + zl, y, c, x)
        z, y, c, x = z % 8, y % 4, c % 2, x % 4
        out.append((i, int(np.ravel_multi_index((z // 4, y, c, x, z % 4), SIZES))))
    return out


def shift(dz=0, dy=0, dc=0, dx=0):
    return pairs_of(lambda z, y, c, x: (z + dz, y + dy, c + dc, x + dx))


def z_window(d):
    if d == 2:
        return pairs_of(lambda z, y, c, x: (z + 2 - 4 * (z % 2), y, c, x))
    return shift(dz=1 if d == 1 else -1)


def back(pairs):
    return [(b, a) for a, b in pairs]


def send(v, pairs):
    return lax.ppermute(v, AXES, pairs)


def expert_at(pos, d, dx):
    return lax.rem(pos[0] + dx, 4) * 4 + lax.rem(pos[1] + d, 4)


def prep_kernel(pos, ids, w, xin, cot, *refs):
    rows, ogs, sel_out = refs[:4], refs[4:8], refs[8]
    rank_s, wt_s, s1, s2, sw2 = refs[9:]
    tok = ids.shape[1]
    eid = lax.broadcasted_iota(jnp.int32, (16, tok), 0)
    member = jnp.zeros((16, tok), F32)
    weight = jnp.zeros((16, tok), F32)
    for k in range(3):
        hit = eid == ids[k : k + 1, :]
        member = member + jnp.where(hit, 1.0, 0.0)
        weight = weight + jnp.where(hit, w[k : k + 1, :].astype(F32), 0.0)
    before = jnp.where(
        lax.broadcasted_iota(jnp.int32, (tok, tok), 0)
        < lax.broadcasted_iota(jnp.int32, (tok, tok), 1),
        1.0,
        0.0,
    )
    rank = jnp.dot(member.astype(BF), before.astype(BF), preferred_element_type=F32)
    rank_s[...] = jnp.where(member > 0.0, rank + 1.0, 0.0)
    wt_s[...] = weight
    nth = lax.broadcasted_iota(jnp.int32, (CAP, tok), 0).astype(F32) + 1.0
    for d in range(4):
        for dx in range(4):
            e = expert_at(pos, d, dx)
            hit = nth == rank_s[pl.ds(e, 1), :]
            one = jnp.where(hit, 1.0, 0.0)
            s1[pl.ds((d * 4 + dx) * CAP, CAP), :] = one
            s2[pl.ds((dx * 4 + d) * CAP, CAP), :] = one
            sw2[pl.ds((dx * 4 + d) * CAP, CAP), :] = jnp.where(hit, wt_s[pl.ds(e, 1), :], 0.0)
    sel1 = s1[...].astype(BF)
    sel_out[...] = s2[...].astype(BF)
    xv = jnp.dot(sel1, xin[...], preferred_element_type=F32).astype(BF)
    cv = jnp.dot(sw2[...].astype(BF), cot[...], preferred_element_type=F32).astype(BF)
    for i in range(4):
        rows[i][...] = xv[i * BLOCK : (i + 1) * BLOCK, :]
        ogs[i][...] = cv[i * BLOCK : (i + 1) * BLOCK, :]


SMEM = pl.BlockSpec(memory_space=pltpu.SMEM)
VMEM = pl.BlockSpec(memory_space=pltpu.VMEM)


def params(mib=16):
    return pltpu.CompilerParams(vmem_limit_bytes=mib * 1024 * 1024)


def call(kernel, args, in_specs, out_shape, out_specs, deps=(), **kw):
    n, m = len(args), len(deps)

    def body(*refs):
        kernel(*refs[:n], *refs[n + m :])

    specs = list(in_specs) + [pl.BlockSpec(memory_space=pl.ANY)] * m
    kw.setdefault("compiler_params", params())
    return pl.pallas_call(body, out_shape=out_shape, in_specs=specs, out_specs=out_specs, **kw)(
        *args, *deps
    )


def cost(flops, nbytes):
    return pl.CostEstimate(flops=int(flops) // 64, bytes_accessed=int(nbytes) // 64, transcendentals=0)


def prep(pos, ids_t, w_t, xin, cot, deps):
    tok, feat = xin.shape
    blk = jax.ShapeDtypeStruct((BLOCK, feat), BF)
    sel = jax.ShapeDtypeStruct((SLOTS, tok), BF)
    return call(
        prep_kernel,
        (pos, ids_t, w_t, xin, cot),
        [SMEM, VMEM, VMEM, VMEM, VMEM],
        [blk] * 8 + [sel],
        [VMEM] * 9,
        deps,
        scratch_shapes=[pltpu.VMEM((16, tok), F32)] * 2 + [pltpu.VMEM((SLOTS, tok), F32)] * 3,
        compiler_params=params(28),
        cost_estimate=cost(4 * SLOTS * tok * feat, 4 * SLOTS * feat + 4 * tok * feat),
        name="prep",
    )


def regroup_values(vals, j):
    return jnp.concatenate([v[j * CAP : (j + 1) * CAP, :] for v in vals], axis=0)


def regroup_kernel(*refs):
    vals = [r[...] for r in refs[:4]]
    for j in range(4):
        refs[4 + j][...] = regroup_values(vals, j)


def regroup(blocks, tile, deps=()):
    width = blocks[0].shape[1]
    spec = pl.BlockSpec((BLOCK, tile), lambda i: (0, i))
    return call(
        regroup_kernel,
        blocks,
        [spec] * 4,
        [jax.ShapeDtypeStruct((BLOCK, width), BF)] * 4,
        [spec] * 4,
        deps,
        grid=(width // tile,),
        cost_estimate=cost(0, 4 * SLOTS * width),
        name="regroup",
    )


def pair_kernel(own, far, out):
    for k in range(4):
        out[k, 0] = own[...]
        out[k, 1] = far[...]


def pair_parts(own, far, deps):
    return call(
        pair_kernel,
        (own, far),
        [VMEM] * 2,
        jax.ShapeDtypeStruct((4, 2) + own.shape, BF),
        VMEM,
        deps,
        cost_estimate=cost(0, 20 * own.size),
        name="pair_parts",
    )


def stack_kernel(pos, *refs):
    vals = [r[...] for r in refs[:4]]
    for j in range(4):
        refs[4][lax.rem(pos[0] - j + 4, 4)] = regroup_values(vals, j)


def regroup_stacked(pos, blocks, tile, deps):
    width = blocks[0].shape[1]
    return call(
        stack_kernel,
        (pos, *blocks),
        [SMEM] + [pl.BlockSpec((BLOCK, tile), lambda i: (0, i))] * 4,
        jax.ShapeDtypeStruct((4, BLOCK, width), BF),
        pl.BlockSpec((4, BLOCK, tile), lambda i: (0, 0, i)),
        deps,
        grid=(width // tile,),
        cost_estimate=cost(0, 4 * SLOTS * width),
        name="regroup",
    )


def assemble_kernel(*refs):
    x_out, og_out = refs[8], refs[9]
    x_out[...] = jnp.concatenate([r[...] for r in refs[:4]], axis=0)
    vals = [r[...] for r in refs[4:8]]
    og_out[...] = jnp.concatenate([regroup_values(vals, j) for j in range(4)], axis=0)


def assemble(xs, ogs, deps):
    width = xs[0].shape[1]
    tile = 512
    spec = pl.BlockSpec((BLOCK, tile), lambda i: (0, i))
    out = pl.BlockSpec((SLOTS, tile), lambda i: (0, i))
    return call(
        assemble_kernel,
        (*xs, *ogs),
        [spec] * 8,
        [jax.ShapeDtypeStruct((SLOTS, width), BF)] * 2,
        [out] * 2,
        deps,
        grid=(width // tile,),
        cost_estimate=cost(0, 8 * SLOTS * width),
        name="assemble",
    )


def hold(arrays, deps):
    anys = pl.BlockSpec(memory_space=pl.ANY)
    count = len(arrays)
    return call(
        lambda *refs: None,
        arrays,
        [anys] * count,
        [jax.ShapeDtypeStruct(v.shape, v.dtype) for v in arrays],
        [anys] * count,
        deps,
        input_output_aliases={k: k for k in range(count)},
        name="hold",
    )


def up_kernel(x, wg, wu, hidden, ca, cb):
    xv = x[...]
    gate = jnp.dot(xv, wg[0], preferred_element_type=F32)
    up = jnp.dot(xv, wu[0], preferred_element_type=F32)
    s = jax.nn.sigmoid(gate)
    silu = gate * s
    hidden[...] = (silu * up).astype(BF)
    ca[...] = up * s * (1.0 + gate * (1.0 - s))
    cb[...] = silu


def up_part(x, w):
    slots, feat = x.shape
    hid = w.shape[2] // 2
    tile = 256
    steps = hid // tile
    out = pl.BlockSpec((slots, tile), lambda i: (0, i))
    return pl.pallas_call(
        up_kernel,
        grid=(steps,),
        out_shape=[
            jax.ShapeDtypeStruct((slots, hid), BF),
            jax.ShapeDtypeStruct((slots, hid), F32),
            jax.ShapeDtypeStruct((slots, hid), F32),
        ],
        in_specs=[
            pl.BlockSpec((slots, feat), lambda i: (0, 0)),
            pl.BlockSpec((1, feat, tile), lambda i: (0, 0, i)),
            pl.BlockSpec((1, feat, tile), lambda i: (0, 0, i + steps)),
        ],
        out_specs=[out] * 3,
        compiler_params=params(46),
        cost_estimate=cost(4 * slots * feat * hid, 4 * feat * hid + 2 * slots * feat),
        name="up_part",
    )(x, w, w)


def down_kernel(part, *refs):
    pos, og, w_own, w_other, hidden, ca, cb = refs[:7]
    pg, pu, dots, wbuf, acc, hv, av, bv, sems = refs[-9:]
    b = pl.program_id(0)
    moves = [
        pltpu.make_async_copy(src, dst, sems.at[k])
        for k, (src, dst) in enumerate(((hidden, hv), (ca, av), (cb, bv)))
    ]

    @pl.when(b == 0)
    def _():
        for m in moves:
            m.start()
        acc[...] = jnp.zeros_like(acc)

    c = pos[4]
    for j in range(2):
        own = pl.multiple_of((2 * j + c) * part, 32)
        other = pl.multiple_of((2 * j + 1 - c) * part, 32)
        wbuf[pl.ds(own, part), :] = w_own[j, 0]
        wbuf[pl.ds(other, part), :] = w_other[j, 0]
    acc[...] += jnp.dot(og[...], wbuf[...], preferred_element_type=F32)

    @pl.when(b == pl.num_programs(0) - 1)
    def _():
        for m in moves:
            m.wait()
        hg = acc[...]
        pg[...] = (hg * av[...]).astype(BF)
        pu[...] = (hg * bv[...]).astype(BF)
        part_dots = jnp.sum(hg * hv[...].astype(F32), axis=1, keepdims=True)
        dots[...] = jnp.broadcast_to(part_dots, dots.shape)


def down_part(pos, og, w_own, w_other, hidden, ca, cb, deps):
    slots, feat = og.shape
    hid = hidden.shape[1]
    part = w_own.shape[2]
    w_spec = pl.BlockSpec(
        (2, 1, part, hid), lambda b, p: (lax.rem(b, 2), lax.rem(lax.div(b, 2) + p[2], 2), 0, 0)
    )
    anys = pl.BlockSpec(memory_space=pl.ANY)
    whole = lambda *shape: pl.BlockSpec(shape, lambda b, p: (0,) * len(shape))
    return pl.pallas_call(
        functools.partial(down_kernel, part),
        out_shape=[
            jax.ShapeDtypeStruct((slots, hid), BF),
            jax.ShapeDtypeStruct((slots, hid), BF),
            jax.ShapeDtypeStruct((slots, 128), F32),
        ],
        grid_spec=pltpu.PrefetchScalarGridSpec(
            num_scalar_prefetch=1,
            grid=(4,),
            in_specs=[pl.BlockSpec((slots, 4 * part), lambda b, p: (0, b)), w_spec, w_spec]
            + [anys] * (3 + len(deps)),
            out_specs=[whole(slots, hid), whole(slots, hid), whole(slots, 128)],
            scratch_shapes=[
                pltpu.VMEM((4 * part, hid), BF),
                pltpu.VMEM((slots, hid), F32),
                pltpu.VMEM((slots, hid), BF),
                pltpu.VMEM((slots, hid), F32),
                pltpu.VMEM((slots, hid), F32),
                pltpu.SemaphoreType.DMA((3,)),
            ],
        ),
        compiler_params=params(28),
        cost_estimate=cost(2 * slots * feat * hid, 2 * feat * hid + 2 * slots * feat),
        name="down_part",
    )(pos, og, w_own, w_other, hidden, ca, cb, *deps)


CONTRACT_LAST = (((1,), (1,)), ((), ()))
CONTRACT_FIRST = (((0,), (0,)), ((), ()))


def row_kernel(tile, pg, pu, w, dots, *outs):
    i = pl.program_id(0)
    hid = pg.shape[1]
    g = lax.dot_general(pg[...], w[0, :, :hid], CONTRACT_LAST, preferred_element_type=F32)
    g = g + lax.dot_general(pu[...], w[0, :, hid:], CONTRACT_LAST, preferred_element_type=F32)
    g = g.astype(BF)
    at = pl.ds(pl.multiple_of(i * tile, tile), tile)
    vals = [g[j * BLOCK : (j + 1) * BLOCK, :] for j in range(4)]
    for j in range(4):
        outs[j][:, at] = regroup_values(vals, j)

    @pl.when(i == 0)
    def _():
        dv = dots[...]
        hi = dv.astype(BF)
        lo = (dv - hi.astype(F32)).astype(BF)
        lane = lax.broadcasted_iota(jnp.int32, dv.shape, 1)
        both = jnp.where(lane == 0, hi.astype(F32), lo.astype(F32)).astype(BF)
        cols = outs[0].shape[1] - 128
        parts = [both[j * BLOCK : (j + 1) * BLOCK, :] for j in range(4)]
        for j in range(4):
            outs[j][:, cols:] = regroup_values(parts, j)


def row_part(pg, pu, w, dots, deps):
    slots, hid = pg.shape
    feat = w.shape[1]
    tile = 256
    whole = lambda *shape: pl.BlockSpec(shape, lambda i: (0,) * len(shape))
    return call(
        functools.partial(row_kernel, tile),
        (pg, pu, w, dots),
        [
            whole(slots, hid),
            whole(slots, hid),
            pl.BlockSpec((1, tile, 2 * hid), lambda i: (0, i, 0)),
            whole(slots, 128),
        ],
        [jax.ShapeDtypeStruct((BLOCK, feat + 128), BF)] * 4,
        [whole(BLOCK, feat + 128)] * 4,
        deps,
        grid=(feat // tile,),
        compiler_params=params(24),
        cost_estimate=cost(4 * slots * feat * hid, 4 * feat * hid + 6 * slots * hid),
        name="row_part",
    )


def grad_kernel(part, pos, left, *refs):
    rights, mine, other, buf, sems = refs[:-4], refs[-4], refs[-3], refs[-2], refs[-1]
    b = pl.program_id(0)
    slot = lax.rem(b, 2)

    def finish(which):
        for u in range(4):
            pltpu.make_async_copy(buf.at[which, u], mine.at[0], sems.at[which, u]).wait()

    @pl.when(b >= 2)
    def _():
        finish(slot)

    lv = left[...].T
    for k, right in enumerate(rights):
        res = jnp.dot(lv, right[...], preferred_element_type=F32).astype(BF)
        cols = slice(k * res.shape[1], (k + 1) * res.shape[1])
        for u in range(4):
            buf[slot, u, :, cols] = res[u * part : (u + 1) * part, :]

    def out(c):
        for u in range(4):
            to = mine if u % 2 == c else other
            at = pos[5 + b * 2 + u // 2]
            pltpu.make_async_copy(buf.at[slot, u], to.at[at], sems.at[slot, u]).start()

    pl.when(pos[4] == 0)(lambda: out(0))
    pl.when(pos[4] == 1)(lambda: out(1))

    @pl.when(b == pl.num_programs(0) - 1)
    def _():
        finish(1 - slot)
        finish(slot)


def grad_part(pos, left, rights, deps=()):
    slots, feat = left.shape
    cols = sum(r.shape[1] for r in rights)
    part = feat // 16
    return call(
        functools.partial(grad_kernel, part),
        (pos, left, *rights),
        [SMEM, pl.BlockSpec((slots, 4 * part), lambda i: (0, i))]
        + [pl.BlockSpec(r.shape, lambda i: (0, 0)) for r in rights],
        [jax.ShapeDtypeStruct((8, part, cols), BF)] * 2,
        [pl.BlockSpec(memory_space=pl.ANY)] * 2,
        deps,
        grid=(4,),
        scratch_shapes=[pltpu.VMEM((2, 4, part, cols), BF), pltpu.SemaphoreType.DMA((2, 4))],
        compiler_params=params(24),
        cost_estimate=cost(2 * slots * feat * cols, 2 * feat * cols + 2 * slots * feat),
        name="grad_part",
    )


def plus(*vals):
    return sum(v.astype(F32) for v in vals)


def first_kernel(mine, got, up, down):
    total = plus(mine[...], got[...]).astype(BF)
    up[...] = total[:2]
    down[...] = total[2:]


def second_kernel(mine, got, up1, dn1, up, down):
    total = plus(mine[...], got[...])
    up[...] = plus(total[0], up1[0]).astype(BF)
    down[...] = plus(total[1], dn1[0]).astype(BF)


def far_kernel(mine, got, up1, dn1, up2, dn2, out, kept):
    out[...] = plus(mine[1], got[1], up1[0], dn2[...]).astype(BF)
    kept[...] = plus(mine[0], got[0], dn1[0], up2[...])


def last_kernel(kept, far, out):
    out[...] = plus(kept[...], far[...]).astype(BF)


def pieces(shape, count, at, tile):
    return pl.BlockSpec((count,) + shape[1:-1] + (tile,), lambda i: (at, 0, i))


def sums(kernel, args, specs, outs, deps, name):
    tile = 384
    cols = args[0].shape[-1]
    flat = pl.BlockSpec((args[0].shape[-2], tile), lambda i: (0, i))
    nbytes = sum(2 * (sp[0] if sp else 1) * args[0].shape[-2] * cols for sp in specs)
    return call(
        kernel,
        args,
        [flat if sp is None else pieces(a.shape, sp[0], sp[1], tile) for a, sp in zip(args, specs)],
        outs,
        [flat if len(o.shape) == 2 else pieces(o.shape, o.shape[0], 0, tile) for o in outs],
        deps,
        grid=(cols // tile,),
        cost_estimate=cost(0, 2 * nbytes),
        name=name,
    )


def shape_of(a, count=None):
    return jax.ShapeDtypeStruct(((count,) if count else ()) + a.shape[1:], BF)


def first_sum(mine, got, deps):
    args, outs = (mine, got), [shape_of(mine, 2)] * 2
    up, down = sums(first_kernel, args, [(4, 0)] * 2, outs, deps, "first_sum")
    return send(up, shift(dy=1)), send(down, shift(dy=-1)), [up]


def second_sum(mine, got, up1, dn1, deps):
    args, outs = (mine, got, up1, dn1), [shape_of(mine)] * 2
    specs = [(2, 2), (2, 2), (1, 0), (1, 0)]
    up, down = sums(second_kernel, args, specs, outs, deps, "second_sum")
    return send(up, shift(dy=1)), send(down, shift(dy=-1)), [up]


def far_sum(mine, got, up1, dn1, up2, dn2, deps):
    args = (mine, got, up1, dn1, up2, dn2)
    outs = [shape_of(mine), jax.ShapeDtypeStruct(mine.shape[1:], F32)]
    specs = [(2, 3), (2, 3), (1, 1), (1, 1), None, None]
    out, kept = sums(far_kernel, args, specs, outs, deps, "far_sum")
    return send(out, shift(dz=4)), kept, [out]


def last_sum(kept, far, deps):
    (out,) = sums(last_kernel, (kept, far), [None] * 2, [shape_of(kept[None])], deps, "last_sum")
    return out


def final_kernel(pos, ids, w, sel, back, grad, gate):
    feat = grad.shape[1]
    acc = jnp.zeros(grad.shape, F32)
    sv = sel[...].astype(F32)
    gates = [jnp.zeros((1, grad.shape[0]), F32) for _ in range(3)]
    for j in range(4):
        at = lax.rem(pos[0] + j, 4)
        part = sv[j * BLOCK : (j + 1) * BLOCK, :]
        acc += lax.dot_general(
            part.astype(BF), back[at, :, :feat], CONTRACT_FIRST, preferred_element_type=F32
        )
        tail = back[at, :, feat:].astype(F32)
        found = part * (tail[:, 0:1] + tail[:, 1:2])
        for d in range(4):
            val = jnp.sum(found[d * CAP : (d + 1) * CAP, :], axis=0, keepdims=True)
            e = expert_at(pos, d, j)
            for k in range(3):
                gates[k] += jnp.where(ids[k : k + 1, :] == e, val, 0.0)
    grad[...] = acc.astype(BF)
    for k in range(3):
        gate[k : k + 1, :] = (gates[k] / w[k : k + 1, :].astype(F32)).astype(BF)


def final(pos, ids_t, w_t, sel, back, feat, deps):
    tok = ids_t.shape[1]
    return call(
        final_kernel,
        (pos, ids_t, w_t, sel, back),
        [SMEM] + [VMEM] * 4,
        [jax.ShapeDtypeStruct((tok, feat), BF), jax.ShapeDtypeStruct((3, tok), BF)],
        [VMEM] * 2,
        deps,
        cost_estimate=cost(2 * SLOTS * tok * feat, 2 * SLOTS * feat + 2 * tok * feat),
        name="final",
    )


def on_device(layer_inputs, cotangent, expert_ids, route_weights, w_gate_up, w_down):
    feat = layer_inputs.shape[1]
    zh, y, c, x, zl = (lax.axis_index(a) for a in AXES)
    places = jnp.zeros((8,), jnp.int32)
    unit = jnp.arange(8, dtype=jnp.int32)
    rel = ((unit % 4 - y) % 4) * 2 + (unit // 4 + zh) % 2
    for (dy, dzh), at in PLACE.items():
        places = jnp.where(rel == dy * 2 + dzh, at, places)
    pos = jnp.concatenate([jnp.stack([x, zl, zh, y, c]).astype(jnp.int32), places])
    ids_t, w_t = expert_ids.T, route_weights.T

    wd = w_down[0].T
    wd_far = send(wd, shift(dz=4))
    made = prep(pos, ids_t, w_t, layer_inputs, cotangent, [])
    rows, ogs, sel = made[:4], made[4:8], made[8]
    z_moves = [z_window(d) for d in (1, 2, 3)]
    x_moves = [shift(dx=d) for d in (1, 2, 3)]

    def over(blocks, moves):
        got = {d: send(blocks[d], moves[d - 1]) for d in (1, 3, 2)}
        return [blocks[0]] + [got[d] for d in (1, 2, 3)]

    home = lambda blocks, moves: over(blocks, [back(m) for m in moves])
    flip = lambda v: send(v, shift(dc=1))
    rows = over([rows[0], *hold(list(rows[1:]), [wd_far])], z_moves)
    pairs = pair_parts(wd, wd_far, [rows[1]])
    rows = regroup(rows, 512, [pairs])
    wd_own = lax.all_to_all(pairs, "y", 0, 0, tiled=True)
    ogs = regroup(over(ogs, x_moves), 512, [rows[0]])
    xs, og = assemble(over(rows, x_moves), over(ogs, z_moves), [])
    (wd_own,) = hold([wd_own], [xs])
    wd_other = flip(wd_own)

    hidden, ca, cb = up_part(xs, w_gate_up)
    pg, pu, dots = down_part(pos, og, wd_own, wd_other, hidden, ca, cb, [])
    g_own, other = grad_part(pos, xs, [pg, pu])
    g_got = flip(other)
    d_own, other = grad_part(pos, og, [hidden], [g_own])
    d_got = flip(other)
    g_up1, g_dn1, dep = first_sum(g_own, g_got, [d_own])
    d_up1, d_dn1, dep = first_sum(d_own, d_got, dep)
    row_grads = row_part(pg, pu, w_gate_up, dots, dep)
    g_up2, g_dn2, dep = second_sum(g_own, g_got, g_up1, g_dn1, [row_grads[0]])
    g_far, g_kept, dep = far_sum(g_own, g_got, g_up1, g_dn1, g_up2, g_dn2, dep)
    back_rows = regroup_stacked(pos, home(row_grads, z_moves), (feat + 128) // 3, dep)
    back_rows_x = lax.all_to_all(back_rows, "x", 0, 0, tiled=True)
    d_up2, d_dn2, dep = second_sum(d_own, d_got, d_up1, d_dn1, [back_rows])
    gu_grad = last_sum(g_kept, g_far, dep)
    d_far, d_kept, dep = far_sum(d_own, d_got, d_up1, d_dn1, d_up2, d_dn2, [gu_grad])
    input_grad, gate_grad = final(pos, ids_t, w_t, sel, back_rows_x, feat, dep)
    down_grad = last_sum(d_kept, d_far, [input_grad])
    return (input_grad, gate_grad.T, gu_grad[None], down_grad.T[None])


def solution(mesh):
    grid = Mesh(mesh.devices.reshape(SIZES), AXES)
    dp, ex = AXES[:3], AXES[3:]
    return jax.shard_map(
        on_device,
        mesh=grid,
        in_specs=(
            P(AXES, None),
            P(AXES, None),
            P(AXES, None),
            P(AXES, None),
            P(ex, None, None),
            P(ex, None, dp),
        ),
        out_specs=(
            P(AXES, None),
            P(AXES, None),
            P(ex, dp, None),
            P(ex, None, dp),
        ),
        check_vma=False,
    )
```

```python
import functools

import jax
import jax.numpy as jnp
import numpy as np
from jax import lax
from jax.experimental import pallas as pl
from jax.experimental.pallas import tpu as pltpu
from jax.sharding import Mesh
from jax.sharding import PartitionSpec as P

AXES = ("zh", "y", "c", "x", "zl")
SIZES = (2, 4, 2, 4, 4)
CAP = 26
BLOCK = 4 * CAP
SLOTS = 16 * CAP
BF = jnp.bfloat16
F32 = jnp.float32
PLACE = {(2, 0): 0, (1, 1): 1, (2, 1): 2, (3, 0): 3, (1, 0): 4, (3, 1): 5, (0, 0): 6, (0, 1): 7}


def pairs_of(move):
    out = []
    for i in range(int(np.prod(SIZES))):
        zh, y, c, x, zl = (int(v) for v in np.unravel_index(i, SIZES))
        z, y, c, x = move(zh * 4 + zl, y, c, x)
        z, y, c, x = z % 8, y % 4, c % 2, x % 4
        out.append((i, int(np.ravel_multi_index((z // 4, y, c, x, z % 4), SIZES))))
    return out


def shift(dz=0, dy=0, dc=0, dx=0):
    return pairs_of(lambda z, y, c, x: (z + dz, y + dy, c + dc, x + dx))


def z_window(d):
    if d == 2:
        return pairs_of(lambda z, y, c, x: (z + 2 - 4 * (z % 2), y, c, x))
    return shift(dz=1 if d == 1 else -1)


def back(pairs):
    return [(b, a) for a, b in pairs]


def send(v, pairs):
    return lax.ppermute(v, AXES, pairs)


def expert_at(pos, d, dx):
    return lax.rem(pos[0] + dx, 4) * 4 + lax.rem(pos[1] + d, 4)


def prep_kernel(pos, ids, w, xin, cot, *refs):
    rows, ogs, sel_out = refs[:4], refs[4:8], refs[8]
    rank_s, wt_s, s1, s2, sw2 = refs[9:]
    tok = ids.shape[1]
    eid = lax.broadcasted_iota(jnp.int32, (16, tok), 0)
    member = jnp.zeros((16, tok), F32)
    weight = jnp.zeros((16, tok), F32)
    for k in range(3):
        hit = eid == ids[k : k + 1, :]
        member = member + jnp.where(hit, 1.0, 0.0)
        weight = weight + jnp.where(hit, w[k : k + 1, :].astype(F32), 0.0)
    before = jnp.where(
        lax.broadcasted_iota(jnp.int32, (tok, tok), 0)
        < lax.broadcasted_iota(jnp.int32, (tok, tok), 1),
        1.0,
        0.0,
    )
    rank = jnp.dot(member.astype(BF), before.astype(BF), preferred_element_type=F32)
    rank_s[...] = jnp.where(member > 0.0, rank + 1.0, 0.0)
    wt_s[...] = weight
    nth = lax.broadcasted_iota(jnp.int32, (CAP, tok), 0).astype(F32) + 1.0
    for d in range(4):
        for dx in range(4):
            e = expert_at(pos, d, dx)
            hit = nth == rank_s[pl.ds(e, 1), :]
            one = jnp.where(hit, 1.0, 0.0)
            s1[pl.ds((d * 4 + dx) * CAP, CAP), :] = one
            s2[pl.ds((dx * 4 + d) * CAP, CAP), :] = one
            sw2[pl.ds((dx * 4 + d) * CAP, CAP), :] = jnp.where(hit, wt_s[pl.ds(e, 1), :], 0.0)
    sel1 = s1[...].astype(BF)
    sel_out[...] = s2[...].astype(BF)
    xv = jnp.dot(sel1, xin[...], preferred_element_type=F32).astype(BF)
    cv = jnp.dot(sw2[...].astype(BF), cot[...], preferred_element_type=F32).astype(BF)
    for i in range(4):
        rows[i][...] = xv[i * BLOCK : (i + 1) * BLOCK, :]
        ogs[i][...] = cv[i * BLOCK : (i + 1) * BLOCK, :]


SMEM = pl.BlockSpec(memory_space=pltpu.SMEM)
VMEM = pl.BlockSpec(memory_space=pltpu.VMEM)


def params(mib=16):
    return pltpu.CompilerParams(vmem_limit_bytes=mib * 1024 * 1024)


def call(kernel, args, in_specs, out_shape, out_specs, deps=(), **kw):
    n, m = len(args), len(deps)

    def body(*refs):
        kernel(*refs[:n], *refs[n + m :])

    specs = list(in_specs) + [pl.BlockSpec(memory_space=pl.ANY)] * m
    kw.setdefault("compiler_params", params())
    return pl.pallas_call(body, out_shape=out_shape, in_specs=specs, out_specs=out_specs, **kw)(
        *args, *deps
    )


def cost(flops, nbytes):
    return pl.CostEstimate(flops=int(flops) // 64, bytes_accessed=int(nbytes) // 64, transcendentals=0)


def prep(pos, ids_t, w_t, xin, cot, deps):
    tok, feat = xin.shape
    blk = jax.ShapeDtypeStruct((BLOCK, feat), BF)
    sel = jax.ShapeDtypeStruct((SLOTS, tok), BF)
    return call(
        prep_kernel,
        (pos, ids_t, w_t, xin, cot),
        [SMEM, VMEM, VMEM, VMEM, VMEM],
        [blk] * 8 + [sel],
        [VMEM] * 9,
        deps,
        scratch_shapes=[pltpu.VMEM((16, tok), F32)] * 2 + [pltpu.VMEM((SLOTS, tok), F32)] * 3,
        compiler_params=params(28),
        cost_estimate=cost(4 * SLOTS * tok * feat, 4 * SLOTS * feat + 4 * tok * feat),
        name="prep",
    )


def regroup_values(vals, j):
    return jnp.concatenate([v[j * CAP : (j + 1) * CAP, :] for v in vals], axis=0)


def regroup_kernel(*refs):
    vals = [r[...] for r in refs[:4]]
    for j in range(4):
        refs[4 + j][...] = regroup_values(vals, j)


def regroup(blocks, tile, deps=()):
    width = blocks[0].shape[1]
    spec = pl.BlockSpec((BLOCK, tile), lambda i: (0, i))
    return call(
        regroup_kernel,
        blocks,
        [spec] * 4,
        [jax.ShapeDtypeStruct((BLOCK, width), BF)] * 4,
        [spec] * 4,
        deps,
        grid=(width // tile,),
        cost_estimate=cost(0, 4 * SLOTS * width),
        name="regroup",
    )


def pair_kernel(own, far, out):
    for k in range(4):
        out[k, 0] = own[...]
        out[k, 1] = far[...]


def pair_parts(own, far, deps):
    return call(
        pair_kernel,
        (own, far),
        [VMEM] * 2,
        jax.ShapeDtypeStruct((4, 2) + own.shape, BF),
        VMEM,
        deps,
        cost_estimate=cost(0, 20 * own.size),
        name="pair_parts",
    )


def stack_kernel(pos, *refs):
    vals = [r[...] for r in refs[:4]]
    for j in range(4):
        refs[4][lax.rem(pos[0] - j + 4, 4)] = regroup_values(vals, j)


def regroup_stacked(pos, blocks, tile, deps):
    width = blocks[0].shape[1]
    return call(
        stack_kernel,
        (pos, *blocks),
        [SMEM] + [pl.BlockSpec((BLOCK, tile), lambda i: (0, i))] * 4,
        jax.ShapeDtypeStruct((4, BLOCK, width), BF),
        pl.BlockSpec((4, BLOCK, tile), lambda i: (0, 0, i)),
        deps,
        grid=(width // tile,),
        cost_estimate=cost(0, 4 * SLOTS * width),
        name="regroup",
    )


def assemble_kernel(*refs):
    x_out, og_out = refs[8], refs[9]
    x_out[...] = jnp.concatenate([r[...] for r in refs[:4]], axis=0)
    vals = [r[...] for r in refs[4:8]]
    og_out[...] = jnp.concatenate([regroup_values(vals, j) for j in range(4)], axis=0)


def assemble(xs, ogs, deps):
    width = xs[0].shape[1]
    tile = 512
    spec = pl.BlockSpec((BLOCK, tile), lambda i: (0, i))
    out = pl.BlockSpec((SLOTS, tile), lambda i: (0, i))
    return call(
        assemble_kernel,
        (*xs, *ogs),
        [spec] * 8,
        [jax.ShapeDtypeStruct((SLOTS, width), BF)] * 2,
        [out] * 2,
        deps,
        grid=(width // tile,),
        cost_estimate=cost(0, 8 * SLOTS * width),
        name="assemble",
    )


def hold(arrays, deps):
    anys = pl.BlockSpec(memory_space=pl.ANY)
    count = len(arrays)
    return call(
        lambda *refs: None,
        arrays,
        [anys] * count,
        [jax.ShapeDtypeStruct(v.shape, v.dtype) for v in arrays],
        [anys] * count,
        deps,
        input_output_aliases={k: k for k in range(count)},
        name="hold",
    )


def up_kernel(x, wg, wu, hidden, ca, cb):
    xv = x[...]
    gate = jnp.dot(xv, wg[0], preferred_element_type=F32)
    up = jnp.dot(xv, wu[0], preferred_element_type=F32)
    s = jax.nn.sigmoid(gate)
    silu = gate * s
    hidden[...] = (silu * up).astype(BF)
    ca[...] = up * s * (1.0 + gate * (1.0 - s))
    cb[...] = silu


def up_part(x, w):
    slots, feat = x.shape
    hid = w.shape[2] // 2
    tile = 256
    steps = hid // tile
    out = pl.BlockSpec((slots, tile), lambda i: (0, i))
    return pl.pallas_call(
        up_kernel,
        grid=(steps,),
        out_shape=[
            jax.ShapeDtypeStruct((slots, hid), BF),
            jax.ShapeDtypeStruct((slots, hid), F32),
            jax.ShapeDtypeStruct((slots, hid), F32),
        ],
        in_specs=[
            pl.BlockSpec((slots, feat), lambda i: (0, 0)),
            pl.BlockSpec((1, feat, tile), lambda i: (0, 0, i)),
            pl.BlockSpec((1, feat, tile), lambda i: (0, 0, i + steps)),
        ],
        out_specs=[out] * 3,
        compiler_params=params(46),
        cost_estimate=cost(4 * slots * feat * hid, 4 * feat * hid + 2 * slots * feat),
        name="up_part",
    )(x, w, w)


def down_kernel(part, *refs):
    pos, og, w_own, w_other, hidden, ca, cb = refs[:7]
    pg, pu, dots, wbuf, acc, hv, av, bv, sems = refs[-9:]
    b = pl.program_id(0)
    moves = [
        pltpu.make_async_copy(src, dst, sems.at[k])
        for k, (src, dst) in enumerate(((hidden, hv), (ca, av), (cb, bv)))
    ]

    @pl.when(b == 0)
    def _():
        for m in moves:
            m.start()
        acc[...] = jnp.zeros_like(acc)

    c = pos[4]
    for j in range(4):
        own = pl.multiple_of((2 * j + c) * part, 32)
        other = pl.multiple_of((2 * j + 1 - c) * part, 32)
        wbuf[pl.ds(own, part), :] = w_own[j, 0]
        wbuf[pl.ds(other, part), :] = w_other[j, 0]
    acc[...] += jnp.dot(og[...], wbuf[...], preferred_element_type=F32)

    @pl.when(b == pl.num_programs(0) - 1)
    def _():
        for m in moves:
            m.wait()
        hg = acc[...]
        pg[...] = (hg * av[...]).astype(BF)
        pu[...] = (hg * bv[...]).astype(BF)
        part_dots = jnp.sum(hg * hv[...].astype(F32), axis=1, keepdims=True)
        dots[...] = jnp.broadcast_to(part_dots, dots.shape)


def down_part(pos, og, w_own, w_other, hidden, ca, cb, deps):
    slots, feat = og.shape
    hid = hidden.shape[1]
    part = w_own.shape[2]
    w_spec = pl.BlockSpec(
        (4, 1, part, hid), lambda b, p: (0, lax.rem(b + p[2], 2), 0, 0)
    )
    anys = pl.BlockSpec(memory_space=pl.ANY)
    whole = lambda *shape: pl.BlockSpec(shape, lambda b, p: (0,) * len(shape))
    return pl.pallas_call(
        functools.partial(down_kernel, part),
        out_shape=[
            jax.ShapeDtypeStruct((slots, hid), BF),
            jax.ShapeDtypeStruct((slots, hid), BF),
            jax.ShapeDtypeStruct((slots, 128), F32),
        ],
        grid_spec=pltpu.PrefetchScalarGridSpec(
            num_scalar_prefetch=1,
            grid=(2,),
            in_specs=[pl.BlockSpec((slots, 8 * part), lambda b, p: (0, b)), w_spec, w_spec]
            + [anys] * (3 + len(deps)),
            out_specs=[whole(slots, hid), whole(slots, hid), whole(slots, 128)],
            scratch_shapes=[
                pltpu.VMEM((8 * part, hid), BF),
                pltpu.VMEM((slots, hid), F32),
                pltpu.VMEM((slots, hid), BF),
                pltpu.VMEM((slots, hid), F32),
                pltpu.VMEM((slots, hid), F32),
                pltpu.SemaphoreType.DMA((3,)),
            ],
        ),
        compiler_params=params(28),
        cost_estimate=cost(2 * slots * feat * hid, 2 * feat * hid + 2 * slots * feat),
        name="down_part",
    )(pos, og, w_own, w_other, hidden, ca, cb, *deps)


CONTRACT_LAST = (((1,), (1,)), ((), ()))
CONTRACT_FIRST = (((0,), (0,)), ((), ()))


def row_kernel(tile, pg, pu, w, dots, *outs):
    i = pl.program_id(0)
    hid = pg.shape[1]
    g = lax.dot_general(pg[...], w[0, :, :hid], CONTRACT_LAST, preferred_element_type=F32)
    g = g + lax.dot_general(pu[...], w[0, :, hid:], CONTRACT_LAST, preferred_element_type=F32)
    g = g.astype(BF)
    at = pl.ds(pl.multiple_of(i * tile, tile), tile)
    vals = [g[j * BLOCK : (j + 1) * BLOCK, :] for j in range(4)]
    for j in range(4):
        outs[j][:, at] = regroup_values(vals, j)

    @pl.when(i == 0)
    def _():
        dv = dots[...]
        hi = dv.astype(BF)
        lo = (dv - hi.astype(F32)).astype(BF)
        lane = lax.broadcasted_iota(jnp.int32, dv.shape, 1)
        both = jnp.where(lane == 0, hi.astype(F32), lo.astype(F32)).astype(BF)
        cols = outs[0].shape[1] - 128
        parts = [both[j * BLOCK : (j + 1) * BLOCK, :] for j in range(4)]
        for j in range(4):
            outs[j][:, cols:] = regroup_values(parts, j)


def row_part(pg, pu, w, dots, deps):
    slots, hid = pg.shape
    feat = w.shape[1]
    tile = 256
    whole = lambda *shape: pl.BlockSpec(shape, lambda i: (0,) * len(shape))
    return call(
        functools.partial(row_kernel, tile),
        (pg, pu, w, dots),
        [
            whole(slots, hid),
            whole(slots, hid),
            pl.BlockSpec((1, tile, 2 * hid), lambda i: (0, i, 0)),
            whole(slots, 128),
        ],
        [jax.ShapeDtypeStruct((BLOCK, feat + 128), BF)] * 4,
        [whole(BLOCK, feat + 128)] * 4,
        deps,
        grid=(feat // tile,),
        compiler_params=params(24),
        cost_estimate=cost(4 * slots * feat * hid, 4 * feat * hid + 6 * slots * hid),
        name="row_part",
    )


def grad_kernel(part, pos, left, *refs):
    rights, mine, other, buf, sems = refs[:-4], refs[-4], refs[-3], refs[-2], refs[-1]
    b = pl.program_id(0)
    slot = lax.rem(b, 2)

    def finish(which):
        for u in range(4):
            pltpu.make_async_copy(buf.at[which, u], mine.at[0], sems.at[which, u]).wait()

    @pl.when(b >= 2)
    def _():
        finish(slot)

    lv = left[...].T
    for k, right in enumerate(rights):
        res = jnp.dot(lv, right[...], preferred_element_type=F32).astype(BF)
        cols = slice(k * res.shape[1], (k + 1) * res.shape[1])
        for u in range(4):
            buf[slot, u, :, cols] = res[u * part : (u + 1) * part, :]

    def out(c):
        for u in range(4):
            to = mine if u % 2 == c else other
            at = pos[5 + b * 2 + u // 2]
            pltpu.make_async_copy(buf.at[slot, u], to.at[at], sems.at[slot, u]).start()

    pl.when(pos[4] == 0)(lambda: out(0))
    pl.when(pos[4] == 1)(lambda: out(1))

    @pl.when(b == pl.num_programs(0) - 1)
    def _():
        finish(1 - slot)
        finish(slot)


def grad_part(pos, left, rights, deps=()):
    slots, feat = left.shape
    cols = sum(r.shape[1] for r in rights)
    part = feat // 16
    return call(
        functools.partial(grad_kernel, part),
        (pos, left, *rights),
        [SMEM, pl.BlockSpec((slots, 4 * part), lambda i: (0, i))]
        + [pl.BlockSpec(r.shape, lambda i: (0, 0)) for r in rights],
        [jax.ShapeDtypeStruct((8, part, cols), BF)] * 2,
        [pl.BlockSpec(memory_space=pl.ANY)] * 2,
        deps,
        grid=(4,),
        scratch_shapes=[pltpu.VMEM((2, 4, part, cols), BF), pltpu.SemaphoreType.DMA((2, 4))],
        compiler_params=params(24),
        cost_estimate=cost(2 * slots * feat * cols, 2 * feat * cols + 2 * slots * feat),
        name="grad_part",
    )


def plus(*vals):
    return sum(v.astype(F32) for v in vals)


def first_kernel(mine, got, up, down):
    total = plus(mine[...], got[...]).astype(BF)
    up[...] = total[:2]
    down[...] = total[2:]


def second_kernel(mine, got, up1, dn1, up, down):
    total = plus(mine[...], got[...])
    up[...] = plus(total[0], up1[0]).astype(BF)
    down[...] = plus(total[1], dn1[0]).astype(BF)


def far_kernel(mine, got, up1, dn1, up2, dn2, out, kept):
    out[...] = plus(mine[1], got[1], up1[0], dn2[...]).astype(BF)
    kept[...] = plus(mine[0], got[0], dn1[0], up2[...])


def last_kernel(kept, far, out):
    out[...] = plus(kept[...], far[...]).astype(BF)


def pieces(shape, count, at, tile):
    return pl.BlockSpec((count,) + shape[1:-1] + (tile,), lambda i: (at, 0, i))


def sums(kernel, args, specs, outs, deps, name):
    tile = 384
    cols = args[0].shape[-1]
    flat = pl.BlockSpec((args[0].shape[-2], tile), lambda i: (0, i))
    nbytes = sum(2 * (sp[0] if sp else 1) * args[0].shape[-2] * cols for sp in specs)
    return call(
        kernel,
        args,
        [flat if sp is None else pieces(a.shape, sp[0], sp[1], tile) for a, sp in zip(args, specs)],
        outs,
        [flat if len(o.shape) == 2 else pieces(o.shape, o.shape[0], 0, tile) for o in outs],
        deps,
        grid=(cols // tile,),
        cost_estimate=cost(0, 2 * nbytes),
        name=name,
    )


def shape_of(a, count=None):
    return jax.ShapeDtypeStruct(((count,) if count else ()) + a.shape[1:], BF)


def first_sum(mine, got, deps):
    args, outs = (mine, got), [shape_of(mine, 2)] * 2
    up, down = sums(first_kernel, args, [(4, 0)] * 2, outs, deps, "first_sum")
    return send(up, shift(dy=1)), send(down, shift(dy=-1)), [up]


def second_sum(mine, got, up1, dn1, deps):
    args, outs = (mine, got, up1, dn1), [shape_of(mine)] * 2
    specs = [(2, 2), (2, 2), (1, 0), (1, 0)]
    up, down = sums(second_kernel, args, specs, outs, deps, "second_sum")
    return send(up, shift(dy=1)), send(down, shift(dy=-1)), [up]


def far_sum(mine, got, up1, dn1, up2, dn2, deps):
    args = (mine, got, up1, dn1, up2, dn2)
    outs = [shape_of(mine), jax.ShapeDtypeStruct(mine.shape[1:], F32)]
    specs = [(2, 3), (2, 3), (1, 1), (1, 1), None, None]
    out, kept = sums(far_kernel, args, specs, outs, deps, "far_sum")
    return send(out, shift(dz=4)), kept, [out]


def last_sum(kept, far, deps):
    (out,) = sums(last_kernel, (kept, far), [None] * 2, [shape_of(kept[None])], deps, "last_sum")
    return out


def final_kernel(pos, ids, w, sel, back, grad, gate):
    feat = grad.shape[1]
    acc = jnp.zeros(grad.shape, F32)
    sv = sel[...].astype(F32)
    gates = [jnp.zeros((1, grad.shape[0]), F32) for _ in range(3)]
    for j in range(4):
        at = lax.rem(pos[0] + j, 4)
        part = sv[j * BLOCK : (j + 1) * BLOCK, :]
        acc += lax.dot_general(
            part.astype(BF), back[at, :, :feat], CONTRACT_FIRST, preferred_element_type=F32
        )
        tail = back[at, :, feat:].astype(F32)
        found = part * (tail[:, 0:1] + tail[:, 1:2])
        for d in range(4):
            val = jnp.sum(found[d * CAP : (d + 1) * CAP, :], axis=0, keepdims=True)
            e = expert_at(pos, d, j)
            for k in range(3):
                gates[k] += jnp.where(ids[k : k + 1, :] == e, val, 0.0)
    grad[...] = acc.astype(BF)
    for k in range(3):
        gate[k : k + 1, :] = (gates[k] / w[k : k + 1, :].astype(F32)).astype(BF)


def final(pos, ids_t, w_t, sel, back, feat, deps):
    tok = ids_t.shape[1]
    return call(
        final_kernel,
        (pos, ids_t, w_t, sel, back),
        [SMEM] + [VMEM] * 4,
        [jax.ShapeDtypeStruct((tok, feat), BF), jax.ShapeDtypeStruct((3, tok), BF)],
        [VMEM] * 2,
        deps,
        cost_estimate=cost(2 * SLOTS * tok * feat, 2 * SLOTS * feat + 2 * tok * feat),
        name="final",
    )


def on_device(layer_inputs, cotangent, expert_ids, route_weights, w_gate_up, w_down):
    feat = layer_inputs.shape[1]
    zh, y, c, x, zl = (lax.axis_index(a) for a in AXES)
    places = jnp.zeros((8,), jnp.int32)
    unit = jnp.arange(8, dtype=jnp.int32)
    rel = ((unit % 4 - y) % 4) * 2 + (unit // 4 + zh) % 2
    for (dy, dzh), at in PLACE.items():
        places = jnp.where(rel == dy * 2 + dzh, at, places)
    pos = jnp.concatenate([jnp.stack([x, zl, zh, y, c]).astype(jnp.int32), places])
    ids_t, w_t = expert_ids.T, route_weights.T

    wd = w_down[0].T
    wd_far = send(wd, shift(dz=4))
    made = prep(pos, ids_t, w_t, layer_inputs, cotangent, [])
    rows, ogs, sel = made[:4], made[4:8], made[8]
    z_moves = [z_window(d) for d in (1, 2, 3)]
    x_moves = [shift(dx=d) for d in (1, 2, 3)]

    def over(blocks, moves):
        got = {d: send(blocks[d], moves[d - 1]) for d in (1, 3, 2)}
        return [blocks[0]] + [got[d] for d in (1, 2, 3)]

    home = lambda blocks, moves: over(blocks, [back(m) for m in moves])
    flip = lambda v: send(v, shift(dc=1))
    rows = over([rows[0], *hold(list(rows[1:]), [wd_far])], z_moves)
    pairs = pair_parts(wd, wd_far, [rows[1]])
    rows = regroup(rows, 512, [pairs])
    wd_own = lax.all_to_all(pairs, "y", 0, 0, tiled=True)
    ogs = regroup(over(ogs, x_moves), 512, [rows[0]])
    xs, og = assemble(over(rows, x_moves), over(ogs, z_moves), [])
    (wd_own,) = hold([wd_own], [xs])
    wd_other = flip(wd_own)

    hidden, ca, cb = up_part(xs, w_gate_up)
    pg, pu, dots = down_part(pos, og, wd_own, wd_other, hidden, ca, cb, [])
    g_own, other = grad_part(pos, xs, [pg, pu])
    g_got = flip(other)
    d_own, other = grad_part(pos, og, [hidden], [g_own])
    d_got = flip(other)
    g_up1, g_dn1, dep = first_sum(g_own, g_got, [d_own])
    d_up1, d_dn1, dep = first_sum(d_own, d_got, dep)
    row_grads = row_part(pg, pu, w_gate_up, dots, dep)
    g_up2, g_dn2, dep = second_sum(g_own, g_got, g_up1, g_dn1, [row_grads[0]])
    g_far, g_kept, dep = far_sum(g_own, g_got, g_up1, g_dn1, g_up2, g_dn2, dep)
    back_rows = regroup_stacked(pos, home(row_grads, z_moves), (feat + 128) // 3, dep)
    back_rows_x = lax.all_to_all(back_rows, "x", 0, 0, tiled=True)
    d_up2, d_dn2, dep = second_sum(d_own, d_got, d_up1, d_dn1, [back_rows])
    gu_grad = last_sum(g_kept, g_far, dep)
    d_far, d_kept, dep = far_sum(d_own, d_got, d_up1, d_dn1, d_up2, d_dn2, [gu_grad])
    input_grad, gate_grad = final(pos, ids_t, w_t, sel, back_rows_x, feat, dep)
    down_grad = last_sum(d_kept, d_far, [input_grad])
    return (input_grad, gate_grad.T, gu_grad[None], down_grad.T[None])


def solution(mesh):
    grid = Mesh(mesh.devices.reshape(SIZES), AXES)
    dp, ex = AXES[:3], AXES[3:]
    return jax.shard_map(
        on_device,
        mesh=grid,
        in_specs=(
            P(AXES, None),
            P(AXES, None),
            P(AXES, None),
            P(AXES, None),
            P(ex, None, None),
            P(ex, None, dp),
        ),
        out_specs=(
            P(AXES, None),
            P(AXES, None),
            P(ex, dp, None),
            P(ex, None, dp),
        ),
        check_vma=False,
    )
```
